32 devices in a mesh: chan: 8 (over z, y), tm: 4 (over x, core).
Axes of the slice: x: 2, y: 2, z: 4, core: 2. Of those that a mesh axis runs over, the one named last changes fastest.
Arguments:
- raw: float32 [2, 256, 1024], P(None, 'chan', 'tm'), may hold values from -40 to 40
- alive: int32 [256], P(('chan', 'tm')), may hold values 0 or 1
- seg_start: int32 [2], replicated, may hold values from 0 to 256, as said below
- norm_half: int32 [256], P(('chan', 'tm')), may hold values from 32 to 64, as said below
Outputs:
- corr: bfloat16 [256, 129, 256], P(('chan', 'tm'))
The draws below stay inside these ranges and needn't reach their ends.
Inputs may be any that keep to these rules, and one draw needn't show every extreme that they name: `seg_start`: some segment starts exactly 256 samples into its window. `norm_half`: some channel has half-length 32 and some 64.
All inputs are finite; a program needn't handle non-finite values. No bound on the sum of `alive` on one device may be relied on, other than what follows from the above.
Results may differ from the reference program's by a relative error of at most 0.02.
Values may be sent and summed in bfloat16 or wider, within the bound.
A program may use at most 64 MiB of HBM per device.

```python
import math
import jax
import jax.numpy as jnp
from jax import lax

CH_DEV = 32
T_DEV = 256
SEGS = 2
LAG = 64
C = 256
NT = 1024
BAND_LO = 4
BAND_HI = 409


def draw_raw(key, part):
    key_noise, key_level = jax.random.split(jax.random.fold_in(key, 11), 2)
    block_count = NT // 64
    noise = jnp.clip(jax.random.normal(key_noise, (SEGS, C, NT), jnp.float32), -4.0, 4.0)
    level = jax.random.uniform(key_level, (SEGS, C, block_count), jnp.float32, -2.3, 2.3)
    envelope = jnp.repeat(jnp.exp(level), 64, axis=2)
    return noise * envelope


def draw_seg_start(key, part):
    key_pick, key_value = jax.random.split(jax.random.fold_in(key, 23))
    values = jax.random.randint(key_value, (SEGS,), 0, T_DEV + 1)
    chosen = jax.random.randint(key_pick, (), 0, SEGS)
    return jnp.where(jnp.arange(SEGS) == chosen, T_DEV, values).astype(jnp.int32)


def draw_norm_half(key, part):
    key_value, key_first, key_second = jax.random.split(jax.random.fold_in(key, 37), 3)
    values = jax.random.randint(key_value, (C,), 32, 65)
    top_slot = jax.random.randint(key_first, (), 0, C)
    low_slot = (top_slot + 1 + jax.random.randint(key_second, (), 0, C - 1)) % C
    positions = jnp.arange(C)
    values = jnp.where(positions == top_slot, 64, values)
    values = jnp.where(positions == low_slot, 32, values)
    return values.astype(jnp.int32)


def plant(array, own_key, smallest, largest):
    place = [jax.random.randint(jax.random.fold_in(own_key, axis), (), 0, length) for axis, length in enumerate(array.shape)]
    main_axis = array.shape.index(max(array.shape))
    next_to = place[:main_axis] + [(place[main_axis] + 1) % array.shape[main_axis]] + place[main_axis + 1:]
    return array.at[tuple(place)].set(smallest).at[tuple(next_to)].set(largest)


def setup_inputs(seed: int = 0) -> dict:
    splits = jax.random.split(jax.random.key(seed), 5)
    raw = draw_raw(jax.random.fold_in(splits[4], 71), 0)
    alive = plant((jax.random.randint(splits[1], (C,), 0, 16) < 15).astype(jnp.int32), jax.random.fold_in(splits[1], 1), 0, 1)
    seg_start = draw_seg_start(jax.random.fold_in(splits[4], 71), 0)
    norm_half = draw_norm_half(jax.random.fold_in(splits[4], 71), 0)
    return {"raw": raw, "alive": alive, "seg_start": seg_start, "norm_half": norm_half}


widest = 64
smooth_half = 32
tiny = 1e-05

def window_mean(signal, half_width):
    length = signal.shape[2]
    padded = jnp.pad(jnp.abs(signal), ((0, 0), (0, 0), (widest, widest)))
    running = jnp.cumsum(padded, axis=2)
    running = jnp.concatenate([jnp.zeros(running.shape[:2] + (1,), jnp.float32), running], axis=2)
    moments = jnp.arange(length, dtype=jnp.int32)
    full_shape = signal.shape
    upper_index = jnp.broadcast_to(moments[None, None, :] + half_width[None, :, None] + 1 + widest, full_shape).astype(jnp.int32)
    lower_index = jnp.broadcast_to(moments[None, None, :] - half_width[None, :, None] + widest, full_shape).astype(jnp.int32)
    total = jnp.take_along_axis(running, upper_index, axis=2) - jnp.take_along_axis(running, lower_index, axis=2)
    return total / (2 * half_width[None, :, None] + 1).astype(jnp.float32)

def reference(raw, alive, seg_start, norm_half):
    masked = raw * alive.astype(jnp.float32)[None, :, None]
    pieces = []
    for segment in range(SEGS):
        padded = jnp.pad(masked[segment], ((0, 0), (0, NT)))
        pieces.append(lax.dynamic_slice_in_dim(padded, seg_start[segment].astype(jnp.int32), NT, axis=1))
    signal = jnp.stack(pieces, axis=0)
    level = window_mean(signal, norm_half.astype(jnp.int32))
    normed = signal / (level + tiny)
    spectrum = jnp.fft.rfft(normed, axis=2)
    magnitude = jnp.abs(spectrum)
    reflected = jnp.pad(magnitude, ((0, 0), (0, 0), (smooth_half, smooth_half)), mode='reflect')
    running = jnp.cumsum(reflected, axis=2)
    running = jnp.concatenate([jnp.zeros(running.shape[:2] + (1,), jnp.float32), running], axis=2)
    span_bins = 2 * smooth_half + 1
    smooth = (running[:, :, span_bins:] - running[:, :, :-span_bins]) / span_bins
    bins = jnp.arange(NT // 2 + 1, dtype=jnp.int32)
    band = ((bins >= BAND_LO) & (bins <= BAND_HI)).astype(jnp.float32)
    gain = band[None, None, :] / (smooth + tiny)
    white = (jnp.fft.irfft(spectrum * gain, n=NT, axis=2) * math.sqrt(NT)).astype(jnp.bfloat16)
    wide = white.astype(jnp.float32)
    padded_all = jnp.pad(wide, ((0, 0), (0, 0), (LAG, LAG)))
    block_count = C // CH_DEV
    blocked = jnp.transpose(padded_all.reshape(SEGS, block_count, CH_DEV, NT + 2 * LAG), (1, 0, 2, 3))

    def one_block(block_rows):
        toeplitz = jnp.stack([block_rows[:, :, 2 * LAG - offset:2 * LAG - offset + NT] for offset in range(2 * LAG + 1)], axis=2)
        return jnp.einsum('silu,sju->ilj', toeplitz, wide, precision=lax.Precision.HIGHEST)
    totals = lax.map(one_block, blocked).reshape(C, 2 * LAG + 1, C)
    scaled = totals * (1.0 / math.sqrt(SEGS * NT))
    channel_ids = jnp.arange(C, dtype=jnp.int32)
    keep = channel_ids[:, None, None] != channel_ids[None, None, :]
    return jnp.where(keep, scaled, 0.0).astype(jnp.bfloat16)
```

```python
import math

import jax
import jax.numpy as jnp
from jax import lax
from jax.sharding import PartitionSpec as P

LAG = 64


widest = 64
smooth_half = 32
tiny = 1e-05
radix = 128


def window_mean(signal, half_width):
    length = signal.shape[2]
    half = half_width[None, :, None]
    width = 2 * half + 1
    power = jnp.pad(jnp.abs(signal), ((0, 0), (0, 0), (widest, widest)))

    def ahead(value, by):
        return jnp.pad(value[:, :, by:], ((0, 0), (0, 0), (0, by)))

    total = jnp.zeros_like(power)
    span = 1
    while span <= 2 * widest + 1:
        total = jnp.where((width & span) != 0, power + ahead(total, span), total)
        power = power + ahead(power, span)
        span *= 2
    rest = widest - half
    span = 1
    while span <= widest:
        total = jnp.where((rest & span) != 0, ahead(total, span), total)
        span *= 2
    return total[:, :, :length] / width.astype(jnp.float32)


def phase_table(row_total, col_total, modulus):
    product = (
        jnp.arange(row_total, dtype=jnp.int32)[:, None]
        * jnp.arange(col_total, dtype=jnp.int32)[None, :]
        % modulus
    )
    angle = product.astype(jnp.float32) * (2.0 * math.pi / modulus)
    return (jnp.cos(angle), jnp.sin(angle))


def forward_transform(signal, cos_q, sin_q, cos_p, sin_p, cos_t, sin_t):
    length = signal.shape[1]
    inner = length // radix
    highest = lax.Precision.HIGHEST
    grid = signal.reshape(-1, inner, radix)
    first_re = jnp.einsum("rqp,qk->rkp", grid, cos_q, precision=highest)
    first_im = -jnp.einsum("rqp,qk->rkp", grid, sin_q, precision=highest)
    turned_re = first_re * cos_t + first_im * sin_t
    turned_im = first_im * cos_t - first_re * sin_t
    out_re = jnp.einsum("rkp,pj->rjk", turned_re, cos_p, precision=highest) + jnp.einsum(
        "rkp,pj->rjk", turned_im, sin_p, precision=highest
    )
    out_im = jnp.einsum("rkp,pj->rjk", turned_im, cos_p, precision=highest) - jnp.einsum(
        "rkp,pj->rjk", turned_re, sin_p, precision=highest
    )
    return (out_re.reshape(-1, length), out_im.reshape(-1, length))


def inverse_real(spec_re, spec_im, cos_q, sin_q, cos_p, sin_p, cos_t, sin_t):
    length = spec_re.shape[1]
    inner = length // radix
    highest = lax.Precision.HIGHEST
    grid_re = spec_re.reshape(-1, radix, inner)
    grid_im = spec_im.reshape(-1, radix, inner)
    first_re = jnp.einsum("rjk,jp->rkp", grid_re, cos_p, precision=highest) - jnp.einsum(
        "rjk,jp->rkp", grid_im, sin_p, precision=highest
    )
    first_im = jnp.einsum("rjk,jp->rkp", grid_im, cos_p, precision=highest) + jnp.einsum(
        "rjk,jp->rkp", grid_re, sin_p, precision=highest
    )
    turned_re = first_re * cos_t - first_im * sin_t
    turned_im = first_im * cos_t + first_re * sin_t
    result = jnp.einsum("rkp,kq->rqp", turned_re, cos_q, precision=highest) - jnp.einsum(
        "rkp,kq->rqp", turned_im, sin_q, precision=highest
    )
    return result.reshape(-1, length)


def whiten(normed):
    segs, rows, length = normed.shape
    inner = length // radix
    cos_q, sin_q = phase_table(inner, inner, inner)
    cos_p, sin_p = phase_table(radix, radix, radix)
    cos_t, sin_t = phase_table(inner, radix, length)
    spec_re, spec_im = forward_transform(
        normed.reshape(-1, length), cos_q, sin_q, cos_p, sin_p, cos_t, sin_t
    )
    magnitude = jnp.sqrt(spec_re * spec_re + spec_im * spec_im)
    circular = jnp.concatenate(
        [magnitude[:, length - smooth_half :], magnitude, magnitude[:, :smooth_half]], axis=1
    )
    running = jnp.cumsum(circular, axis=1)
    running = jnp.concatenate([jnp.zeros((running.shape[0], 1), jnp.float32), running], axis=1)
    span_bins = 2 * smooth_half + 1
    smooth = (running[:, span_bins:] - running[:, :-span_bins]) / span_bins
    bins = jnp.arange(length, dtype=jnp.int32)
    folded = jnp.minimum(bins, length - bins)
    band = ((folded >= length // 250) & (folded <= 2 * length // 5)).astype(jnp.float32)
    gain = band[None, :] / (smooth + tiny)
    traces = inverse_real(spec_re * gain, spec_im * gain, cos_q, sin_q, cos_p, sin_p, cos_t, sin_t)
    return (traces * (1.0 / math.sqrt(length))).reshape(segs, rows, length).astype(jnp.bfloat16)


def normalised(gathered, alive, seg_start, norm_half):
    segs, rows, length = gathered.shape
    gathered = gathered * alive.astype(jnp.float32)[None, :, None]
    pieces = []
    for segment in range(segs):
        padded = jnp.pad(gathered[segment], ((0, 0), (0, length)))
        pieces.append(lax.dynamic_slice_in_dim(padded, seg_start[segment], length, axis=1))
    signal = jnp.stack(pieces, axis=0)
    return signal / (window_mean(signal, norm_half) + tiny)


def gathered_plan(raw, alive, seg_start, norm_half):
    segs = raw.shape[0]
    rows = alive.shape[0]
    lag_count = 2 * LAG + 1
    device = lax.axis_index("chan") * lax.axis_size("tm") + lax.axis_index("tm")
    pieces = lax.all_to_all(raw, "tm", split_axis=1, concat_axis=2, tiled=True)
    white = whiten(normalised(pieces, alive, seg_start, norm_half))
    length = white.shape[2]
    everyone = lax.all_gather(white, ("chan", "tm"), axis=1, tiled=True)
    padded = jnp.pad(white, ((0, 0), (0, 0), (LAG, LAG)))
    toeplitz = jnp.stack(
        [padded[:, :, 2 * LAG - lag : 2 * LAG - lag + length] for lag in range(lag_count)], axis=2
    )
    total = jnp.einsum("silt,sjt->ilj", toeplitz, everyone, preferred_element_type=jnp.float32)
    row_ids = device * rows + jnp.arange(rows, dtype=jnp.int32)
    col_ids = jnp.arange(everyone.shape[1], dtype=jnp.int32)
    keep = row_ids[:, None, None] != col_ids[None, None, :]
    scaled = total * (1.0 / math.sqrt(segs * length))
    return jnp.where(keep, scaled, 0.0).astype(jnp.bfloat16)


def solution(mesh):
    return jax.shard_map(
        gathered_plan,
        mesh=mesh,
        in_specs=(P(None, "chan", "tm"), P(("chan", "tm")), P(), P(("chan", "tm"))),
        out_specs=P(("chan", "tm"), None, None),
        check_vma=False,
    )
```

```python
import math

import jax
import jax.numpy as jnp
import ml_dtypes
import numpy as np
from jax import lax
from jax.experimental import pallas as pl
from jax.experimental.pallas import tpu as pltpu
from jax.sharding import PartitionSpec as P

LAG = 64


widest = 64
smooth_half = 32
tiny = 1e-05
radix = 128


def window_mean(signal, half_width):
    length = signal.shape[2]
    half = half_width[None, :, None]
    width = 2 * half + 1
    power = jnp.pad(jnp.abs(signal), ((0, 0), (0, 0), (widest, widest)))

    def ahead(value, by):
        return jnp.pad(value[:, :, by:], ((0, 0), (0, 0), (0, by)))

    total = jnp.zeros_like(power)
    span = 1
    while span <= 2 * widest + 1:
        total = jnp.where((width & span) != 0, power + ahead(total, span), total)
        power = power + ahead(power, span)
        span *= 2
    rest = widest - half
    span = 1
    while span <= widest:
        total = jnp.where((rest & span) != 0, ahead(total, span), total)
        span *= 2
    return total[:, :, :length] / width.astype(jnp.float32)


def phase_table(row_total, col_total, modulus):
    product = (
        jnp.arange(row_total, dtype=jnp.int32)[:, None]
        * jnp.arange(col_total, dtype=jnp.int32)[None, :]
        % modulus
    )
    angle = product.astype(jnp.float32) * (2.0 * math.pi / modulus)
    return (jnp.cos(angle), jnp.sin(angle))


def forward_transform(signal, cos_q, sin_q, cos_p, sin_p, cos_t, sin_t):
    length = signal.shape[1]
    inner = length // radix
    highest = lax.Precision.HIGHEST
    grid = signal.reshape(-1, inner, radix)
    first_re = jnp.einsum("rqp,qk->rkp", grid, cos_q, precision=highest)
    first_im = -jnp.einsum("rqp,qk->rkp", grid, sin_q, precision=highest)
    turned_re = first_re * cos_t + first_im * sin_t
    turned_im = first_im * cos_t - first_re * sin_t
    out_re = jnp.einsum("rkp,pj->rjk", turned_re, cos_p, precision=highest) + jnp.einsum(
        "rkp,pj->rjk", turned_im, sin_p, precision=highest
    )
    out_im = jnp.einsum("rkp,pj->rjk", turned_im, cos_p, precision=highest) - jnp.einsum(
        "rkp,pj->rjk", turned_re, sin_p, precision=highest
    )
    return (out_re.reshape(-1, length), out_im.reshape(-1, length))


def inverse_real(spec_re, spec_im, cos_q, sin_q, cos_p, sin_p, cos_t, sin_t):
    length = spec_re.shape[1]
    inner = length // radix
    highest = lax.Precision.HIGHEST
    grid_re = spec_re.reshape(-1, radix, inner)
    grid_im = spec_im.reshape(-1, radix, inner)
    first_re = jnp.einsum("rjk,jp->rkp", grid_re, cos_p, precision=highest) - jnp.einsum(
        "rjk,jp->rkp", grid_im, sin_p, precision=highest
    )
    first_im = jnp.einsum("rjk,jp->rkp", grid_im, cos_p, precision=highest) + jnp.einsum(
        "rjk,jp->rkp", grid_re, sin_p, precision=highest
    )
    turned_re = first_re * cos_t - first_im * sin_t
    turned_im = first_im * cos_t + first_re * sin_t
    result = jnp.einsum("rkp,kq->rqp", turned_re, cos_q, precision=highest) - jnp.einsum(
        "rkp,kq->rqp", turned_im, sin_q, precision=highest
    )
    return result.reshape(-1, length)


def whiten(normed):
    segs, rows, length = normed.shape
    inner = length // radix
    cos_q, sin_q = phase_table(inner, inner, inner)
    cos_p, sin_p = phase_table(radix, radix, radix)
    cos_t, sin_t = phase_table(inner, radix, length)
    spec_re, spec_im = forward_transform(
        normed.reshape(-1, length), cos_q, sin_q, cos_p, sin_p, cos_t, sin_t
    )
    magnitude = jnp.sqrt(spec_re * spec_re + spec_im * spec_im)
    circular = jnp.concatenate(
        [magnitude[:, length - smooth_half :], magnitude, magnitude[:, :smooth_half]], axis=1
    )
    running = jnp.cumsum(circular, axis=1)
    running = jnp.concatenate([jnp.zeros((running.shape[0], 1), jnp.float32), running], axis=1)
    span_bins = 2 * smooth_half + 1
    smooth = (running[:, span_bins:] - running[:, :-span_bins]) / span_bins
    bins = jnp.arange(length, dtype=jnp.int32)
    folded = jnp.minimum(bins, length - bins)
    band = ((folded >= length // 250) & (folded <= 2 * length // 5)).astype(jnp.float32)
    gain = band[None, :] / (smooth + tiny)
    traces = inverse_real(spec_re * gain, spec_im * gain, cos_q, sin_q, cos_p, sin_p, cos_t, sin_t)
    return (traces * (1.0 / math.sqrt(length))).reshape(segs, rows, length).astype(jnp.bfloat16)


def normalised(gathered, alive, seg_start, norm_half):
    segs, rows, length = gathered.shape
    gathered = gathered * alive.astype(jnp.float32)[None, :, None]
    pieces = []
    for segment in range(segs):
        padded = jnp.pad(gathered[segment], ((0, 0), (0, length)))
        pieces.append(lax.dynamic_slice_in_dim(padded, seg_start[segment], length, axis=1))
    signal = jnp.stack(pieces, axis=0)
    return signal / (window_mean(signal, norm_half) + tiny)


def gathered_plan(raw, alive, seg_start, norm_half):
    segs = raw.shape[0]
    rows = alive.shape[0]
    lag_count = 2 * LAG + 1
    device = lax.axis_index("chan") * lax.axis_size("tm") + lax.axis_index("tm")
    pieces = lax.all_to_all(raw, "tm", split_axis=1, concat_axis=2, tiled=True)
    white = whiten(normalised(pieces, alive, seg_start, norm_half))
    length = white.shape[2]
    everyone = lax.all_gather(white, ("chan", "tm"), axis=1, tiled=True)
    padded = jnp.pad(white, ((0, 0), (0, 0), (LAG, LAG)))
    toeplitz = jnp.stack(
        [padded[:, :, 2 * LAG - lag : 2 * LAG - lag + length] for lag in range(lag_count)], axis=2
    )
    total = jnp.einsum("silt,sjt->ilj", toeplitz, everyone, preferred_element_type=jnp.float32)
    row_ids = device * rows + jnp.arange(rows, dtype=jnp.int32)
    col_ids = jnp.arange(everyone.shape[1], dtype=jnp.int32)
    keep = row_ids[:, None, None] != col_ids[None, None, :]
    scaled = total * (1.0 / math.sqrt(segs * length))
    return jnp.where(keep, scaled, 0.0).astype(jnp.bfloat16)


MESH = pl.DeviceIdType.MESH
lag_rows = 144


def two_parts(table):
    high = table.astype(ml_dtypes.bfloat16)
    low = (table - high.astype(np.float64)).astype(ml_dtypes.bfloat16)
    return np.stack([high, low])


def transform_tables(length):
    half, quarter = length // 2, length // 4
    moments = np.arange(half)
    low_bin, high_bin = length // 250, 2 * length // 5
    ahead, back = [], []
    for parity in range(2):
        bins = 2 * np.arange(quarter) + parity
        angle = 2.0 * np.pi * ((moments[:, None] * bins[None, :]) % length) / length
        ahead.append(np.concatenate([np.cos(angle), -np.sin(angle)], axis=1))
        back.append(np.concatenate([np.cos(angle), -np.sin(angle)], axis=1).T)
    order = np.concatenate([np.arange(0, half, 2), np.arange(1, half, 2)])
    place = np.empty(half, np.int64)
    place[order] = np.arange(half)
    mean = np.zeros((half, half), np.float32)
    for column, bin_index in enumerate(order):
        if low_bin <= bin_index <= high_bin:
            for offset in range(-smooth_half, smooth_half + 1):
                mean[place[abs(bin_index + offset)], column] += 1.0
    return (
        two_parts(np.stack(ahead)),
        two_parts(np.stack(back)),
        mean.astype(ml_dtypes.bfloat16),
    )


def three_parts(value):
    high = value.astype(jnp.bfloat16)
    rest = value - high.astype(jnp.float32)
    middle = rest.astype(jnp.bfloat16)
    low = (rest - middle.astype(jnp.float32)).astype(jnp.bfloat16)
    return jnp.concatenate([high, middle, low], axis=0)


def split_dot(parts, table):
    rows = parts.shape[0] // 3
    result = jnp.dot(parts, table, preferred_element_type=jnp.float32)
    return result[2 * rows :] + result[rows : 2 * rows] + result[:rows]


def table_dot(value, high, low):
    parts = three_parts(value)
    return split_dot(parts, low) + split_dot(parts, high)


def turned(value, by):
    length = value.shape[1]
    return pltpu.roll(value, by % length, 1)


def normed_rows(records, start, alive, half):
    rows, length = records.shape
    signal = records * alive
    bit = 1
    while bit <= length // 4:
        signal = jnp.where((start & bit) != 0, turned(signal, -bit), signal)
        bit *= 2
    lane = lax.broadcasted_iota(jnp.int32, (rows, length), 1)
    signal = jnp.where(lane + start < length, signal, 0.0)
    power = jnp.concatenate([jnp.abs(signal), jnp.zeros((rows, 2 * widest), jnp.float32)], axis=1)
    width = 2 * half + 1
    total = power
    bit = 1
    while bit < 2 * widest:
        power = power + turned(power, -bit)
        bit *= 2
        total = jnp.where((width & bit) != 0, power + turned(total, -bit), total)
    bit = 1
    while bit <= widest:
        total = jnp.where((half & bit) != 0, turned(total, bit), total)
        bit *= 2
    level = total[:, :length] / width.astype(jnp.float32)
    return signal / (level + tiny)


def whiten_rows(normed, ahead, back, mean):
    length = normed.shape[1]
    half, quarter = length // 2, length // 4
    left, right = normed[:, :half], normed[:, half:]
    even = table_dot(left + right, ahead[0, 0], ahead[1, 0])
    odd = table_dot(left - right, ahead[0, 1], ahead[1, 1])
    even_power = even * even
    odd_power = odd * odd
    magnitude = jnp.sqrt(
        jnp.concatenate(
            [
                even_power[:, :quarter] + even_power[:, quarter:],
                odd_power[:, :quarter] + odd_power[:, quarter:],
            ],
            axis=1,
        )
    )
    smooth = split_dot(three_parts(magnitude), mean) / (2 * smooth_half + 1)
    place = lax.broadcasted_iota(jnp.int32, smooth.shape, 1)
    bins = jnp.where(place < quarter, 2 * place, 2 * (place - quarter) + 1)
    keep = (bins >= length // 250) & (bins <= 2 * length // 5)
    gain = jnp.where(keep, 1.0 / (smooth + tiny), 0.0)
    even_gain, odd_gain = gain[:, :quarter], gain[:, quarter:]
    even = even * jnp.concatenate([even_gain, even_gain], axis=1)
    odd = odd * jnp.concatenate([odd_gain, odd_gain], axis=1)
    even = table_dot(even, back[0, 0], back[1, 0])
    odd = table_dot(odd, back[0, 1], back[1, 1])
    return jnp.concatenate([even + odd, even - odd], axis=1) * (2.0 / math.sqrt(length))


def fill_lags(white, target, slot):
    rows, length = white.shape
    ring = jnp.concatenate([white, jnp.zeros((rows, 2 * LAG), jnp.float32)], axis=1)
    ring = turned(ring, -LAG)
    for row in range(rows):
        spread = jnp.broadcast_to(ring[row : row + 1], (lag_rows, length + 2 * LAG))
        lagged = pltpu.roll(spread, 0, 1, stride=1, stride_axis=0)
        target[slot, row] = lagged[:, :length].astype(jnp.bfloat16)


def fused_kernel(
    raw, alive, seg_start, norm_half, ahead_hbm, back_hbm, mean_hbm, out,
    ahead, back, mean, table_sem, records, params, own, other, lagged, totals,
    raw_send, raw_recv, param_send, param_recv, rail_send, rail_recv, core_send, core_recv,
):
    chan, tm = lax.axis_index("chan"), lax.axis_index("tm")
    depth = lax.axis_size("chan") // 2
    groups = lax.axis_size("tm")
    z, y, x, core = chan // 2, chan % 2, tm // 2, tm % 2
    rows = alive.shape[0]
    pair = 2 * rows
    length = own.shape[2]
    blocks = own.shape[0]

    loads = [
        pltpu.make_async_copy(source, target, table_sem.at[index])
        for index, (source, target) in enumerate(
            [(ahead_hbm, ahead), (mean_hbm, mean), (back_hbm, back)]
        )
    ]
    for load in loads:
        load.start()

    others = [(chan, (tm + step) % groups) for step in range(1, groups)]
    along = [(((z + step) % depth) * 2 + y, tm) for step in range(1, depth)]
    plane = [
        (y, 1 - x),
        (1 - y, x),
        (1 - y, 1 - x),
    ]
    plane_devices = [(z * 2 + py, px * 2 + core) for py, px in plane]
    barrier = pltpu.get_barrier_semaphore()
    greeted = others + along + plane_devices[1:]
    for device in greeted:
        pl.semaphore_signal(barrier, inc=1, device_id=device, device_id_type=MESH)

    row_ids = lax.broadcasted_iota(jnp.int32, (rows, 128), 0)
    live = jnp.zeros((rows, 128), jnp.int32)
    half = jnp.zeros((rows, 128), jnp.int32)
    for row in range(rows):
        live = jnp.where(row_ids == row, alive[row], live)
        half = jnp.where(row_ids == row, norm_half[row], half)
    params[core] = jnp.concatenate([live, half], axis=0).astype(jnp.float32)
    pl.semaphore_wait(barrier, len(greeted))

    def remote(source, target, send, receive, device):
        return pltpu.make_async_remote_copy(
            src_ref=source, dst_ref=target, send_sem=send, recv_sem=receive,
            device_id=device, device_id_type=MESH,
        )

    started = []
    for step in range(1, groups):
        peer = (tm + step) % groups
        first = pl.multiple_of((peer // 2) * pair, pair)
        copy = remote(
            raw.at[peer % 2, pl.ds(first, pair)], records.at[tm],
            raw_send.at[step - 1], raw_recv.at[tm], (chan, peer),
        )
        copy.start()
        started.append(copy)
    partner = (chan, x * 2 + 1 - core)
    copy = remote(params.at[core], params.at[core], param_send, param_recv, partner)
    copy.start()
    started.append(copy)
    records[tm] = raw[core, pl.ds(pl.multiple_of(x * pair, pair), pair)]
    for step in range(1, groups):
        peer = (tm + step) % groups
        remote(
            records.at[peer], records.at[peer], raw_send.at[step - 1], raw_recv.at[peer],
            (chan, peer),
        ).wait_recv()
    remote(
        params.at[1 - core], params.at[1 - core], param_send, param_recv, partner
    ).wait_recv()

    gathered = jnp.concatenate([records[group] for group in range(groups)], axis=1)
    live = jnp.concatenate([params[0, :rows], params[1, :rows]], axis=0)[:, :1]
    half = jnp.concatenate([params[0, rows:], params[1, rows:]], axis=0)[:, :1]
    normed = normed_rows(gathered, seg_start[core], live, half.astype(jnp.int32))
    for load in loads:
        load.wait()
    white = whiten_rows(normed, ahead, back, mean[...]).astype(jnp.bfloat16)

    def block_of(bz, by, bx):
        return (bz * 2 + by) * 2 + bx

    def to_core(block):
        copy = remote(
            own.at[block], other.at[block], core_send.at[block], core_recv.at[block], partner
        )
        copy.start()
        started.append(copy)

    def to_plane(block, bz):
        for index, device in enumerate(plane_devices):
            copy = remote(
                own.at[block], own.at[block], rail_send.at[bz, index], rail_recv.at[block], device
            )
            copy.start()
            started.append(copy)

    def arrived(buffer, semaphores, block):
        remote(
            buffer.at[block], buffer.at[block], core_send.at[block], semaphores.at[block], partner
        ).wait_recv()

    mine = block_of(z, y, x)
    own[mine] = white
    for index, device in enumerate(along):
        copy = remote(
            own.at[mine], own.at[mine], rail_send.at[depth, index], rail_recv.at[mine], device
        )
        copy.start()
        started.append(copy)
    to_plane(mine, 0)
    to_core(mine)

    wide = white.astype(jnp.float32)
    fill_lags(jnp.where(core == 0, wide[:rows], wide[rows:]), lagged, 0)

    for step in range(1, depth):
        block = block_of((z + step) % depth, y, x)
        arrived(own, rail_recv, block)
        to_plane(block, step)
        to_core(block)

    arrived(other, core_recv, mine)
    wide = other[mine].astype(jnp.float32)
    fill_lags(jnp.where(core == 0, wide[:rows], wide[rows:]), lagged, 1)

    for step in range(depth):
        for py, px in plane:
            block = block_of((z + step) % depth, py, px)
            arrived(own, rail_recv, block)
            to_core(block)

    def lag_dot(slot, columns):
        return lax.dot_general(
            lagged[slot].reshape(rows * lag_rows, length),
            columns[...].reshape(blocks * pair, length),
            (((1,), (1,)), ((), ())),
            preferred_element_type=jnp.float32,
        )

    totals[...] = lag_dot(0, own)
    for step in range(depth):
        for py, px in [(y, x)] + plane:
            if step == 0 and px is x and py is y:
                continue
            arrived(other, core_recv, block_of((z + step) % depth, py, px))
    totals[...] += lag_dot(1, other)
    lag_count = out.shape[1]
    columns = lax.broadcasted_iota(jnp.int32, (lag_count, blocks * pair), 1)
    first = (chan * groups + tm) * rows
    scale = 1.0 / math.sqrt(2 * length)
    for row in range(rows):
        block = totals[row * lag_rows : row * lag_rows + lag_count]
        out[row] = jnp.where(columns != first + row, block * scale, 0.0).astype(jnp.bfloat16)
    for copy in started:
        copy.wait_send()


def fused_plan(raw, alive, seg_start, norm_half):
    segs, width, span = raw.shape
    groups, chans = lax.axis_size("tm"), lax.axis_size("chan")
    rows = alive.shape[0]
    length = span * groups
    depth = chans // 2
    blocks = chans * 2
    half = length // 2
    ahead, back, mean = transform_tables(length)
    vmem = pl.BlockSpec(memory_space=pltpu.VMEM)
    smem = pl.BlockSpec(memory_space=pltpu.SMEM)
    hbm = pl.BlockSpec(memory_space=pl.ANY)
    dma = pltpu.SemaphoreType.DMA
    return pl.pallas_call(
        fused_kernel,
        out_shape=jax.ShapeDtypeStruct((rows, 2 * LAG + 1, width * chans), jnp.bfloat16),
        in_specs=[vmem, smem, smem, smem, hbm, hbm, hbm],
        out_specs=vmem,
        scratch_shapes=[
            pltpu.VMEM((2, 2, half, half), jnp.bfloat16),
            pltpu.VMEM((2, 2, half, half), jnp.bfloat16),
            pltpu.VMEM((half, half), jnp.bfloat16),
            dma((3,)),
            pltpu.VMEM((groups, 2 * rows, span), jnp.float32),
            pltpu.VMEM((2, 2 * rows, 128), jnp.float32),
            pltpu.VMEM((blocks, 2 * rows, length), jnp.bfloat16),
            pltpu.VMEM((blocks, 2 * rows, length), jnp.bfloat16),
            pltpu.VMEM((2, rows, lag_rows, length), jnp.bfloat16),
            pltpu.VMEM((rows * lag_rows, width * chans), jnp.float32),
            dma((groups - 1,)),
            dma((groups,)),
            dma(()),
            dma(()),
            dma((depth + 1, 3)),
            dma((blocks,)),
            dma((blocks,)),
            dma((blocks,)),
        ],
        compiler_params=pltpu.CompilerParams(
            collective_id=0, has_side_effects=True, vmem_limit_bytes=48 * 1024 * 1024
        ),
        cost_estimate=pl.CostEstimate(
            flops=4 * rows * lag_rows * length * width * chans,
            bytes_accessed=6 * 1024 * 1024,
            transcendentals=0,
        ),
    )(raw, alive, seg_start, norm_half, ahead, back, mean)


def on_device(raw, alive, seg_start, norm_half):
    segs, width, span = raw.shape
    shape = (lax.axis_size("chan"), lax.axis_size("tm"), segs, alive.shape[0], span)
    if shape == (8, 4, 2, 8, 256):
        return fused_plan(raw, alive, seg_start, norm_half)
    return gathered_plan(raw, alive, seg_start, norm_half)


def solution(mesh):
    return jax.shard_map(
        on_device,
        mesh=mesh,
        in_specs=(P(None, "chan", "tm"), P(("chan", "tm")), P(), P(("chan", "tm"))),
        out_specs=P(("chan", "tm"), None, None),
        check_vma=False,
    )
```

```python
import math

import jax
import jax.numpy as jnp
import ml_dtypes
import numpy as np
from jax import lax
from jax.experimental import pallas as pl
from jax.experimental.pallas import tpu as pltpu
from jax.sharding import PartitionSpec as P

LAG = 64


widest = 64
smooth_half = 32
tiny = 1e-05
radix = 128


def window_mean(signal, half_width):
    length = signal.shape[2]
    half = half_width[None, :, None]
    width = 2 * half + 1
    power = jnp.pad(jnp.abs(signal), ((0, 0), (0, 0), (widest, widest)))

    def ahead(value, by):
        return jnp.pad(value[:, :, by:], ((0, 0), (0, 0), (0, by)))

    total = jnp.zeros_like(power)
    span = 1
    while span <= 2 * widest + 1:
        total = jnp.where((width & span) != 0, power + ahead(total, span), total)
        power = power + ahead(power, span)
        span *= 2
    rest = widest - half
    span = 1
    while span <= widest:
        total = jnp.where((rest & span) != 0, ahead(total, span), total)
        span *= 2
    return total[:, :, :length] / width.astype(jnp.float32)


def phase_table(row_total, col_total, modulus):
    product = (
        jnp.arange(row_total, dtype=jnp.int32)[:, None]
        * jnp.arange(col_total, dtype=jnp.int32)[None, :]
        % modulus
    )
    angle = product.astype(jnp.float32) * (2.0 * math.pi / modulus)
    return (jnp.cos(angle), jnp.sin(angle))


def forward_transform(signal, cos_q, sin_q, cos_p, sin_p, cos_t, sin_t):
    length = signal.shape[1]
    inner = length // radix
    highest = lax.Precision.HIGHEST
    grid = signal.reshape(-1, inner, radix)
    first_re = jnp.einsum("rqp,qk->rkp", grid, cos_q, precision=highest)
    first_im = -jnp.einsum("rqp,qk->rkp", grid, sin_q, precision=highest)
    turned_re = first_re * cos_t + first_im * sin_t
    turned_im = first_im * cos_t - first_re * sin_t
    out_re = jnp.einsum("rkp,pj->rjk", turned_re, cos_p, precision=highest) + jnp.einsum(
        "rkp,pj->rjk", turned_im, sin_p, precision=highest
    )
    out_im = jnp.einsum("rkp,pj->rjk", turned_im, cos_p, precision=highest) - jnp.einsum(
        "rkp,pj->rjk", turned_re, sin_p, precision=highest
    )
    return (out_re.reshape(-1, length), out_im.reshape(-1, length))


def inverse_real(spec_re, spec_im, cos_q, sin_q, cos_p, sin_p, cos_t, sin_t):
    length = spec_re.shape[1]
    inner = length // radix
    highest = lax.Precision.HIGHEST
    grid_re = spec_re.reshape(-1, radix, inner)
    grid_im = spec_im.reshape(-1, radix, inner)
    first_re = jnp.einsum("rjk,jp->rkp", grid_re, cos_p, precision=highest) - jnp.einsum(
        "rjk,jp->rkp", grid_im, sin_p, precision=highest
    )
    first_im = jnp.einsum("rjk,jp->rkp", grid_im, cos_p, precision=highest) + jnp.einsum(
        "rjk,jp->rkp", grid_re, sin_p, precision=highest
    )
    turned_re = first_re * cos_t - first_im * sin_t
    turned_im = first_im * cos_t + first_re * sin_t
    result = jnp.einsum("rkp,kq->rqp", turned_re, cos_q, precision=highest) - jnp.einsum(
        "rkp,kq->rqp", turned_im, sin_q, precision=highest
    )
    return result.reshape(-1, length)


def whiten(normed):
    segs, rows, length = normed.shape
    inner = length // radix
    cos_q, sin_q = phase_table(inner, inner, inner)
    cos_p, sin_p = phase_table(radix, radix, radix)
    cos_t, sin_t = phase_table(inner, radix, length)
    spec_re, spec_im = forward_transform(
        normed.reshape(-1, length), cos_q, sin_q, cos_p, sin_p, cos_t, sin_t
    )
    magnitude = jnp.sqrt(spec_re * spec_re + spec_im * spec_im)
    circular = jnp.concatenate(
        [magnitude[:, length - smooth_half :], magnitude, magnitude[:, :smooth_half]], axis=1
    )
    running = jnp.cumsum(circular, axis=1)
    running = jnp.concatenate([jnp.zeros((running.shape[0], 1), jnp.float32), running], axis=1)
    span_bins = 2 * smooth_half + 1
    smooth = (running[:, span_bins:] - running[:, :-span_bins]) / span_bins
    bins = jnp.arange(length, dtype=jnp.int32)
    folded = jnp.minimum(bins, length - bins)
    band = ((folded >= length // 250) & (folded <= 2 * length // 5)).astype(jnp.float32)
    gain = band[None, :] / (smooth + tiny)
    traces = inverse_real(spec_re * gain, spec_im * gain, cos_q, sin_q, cos_p, sin_p, cos_t, sin_t)
    return (traces * (1.0 / math.sqrt(length))).reshape(segs, rows, length).astype(jnp.bfloat16)


def normalised(gathered, alive, seg_start, norm_half):
    segs, rows, length = gathered.shape
    gathered = gathered * alive.astype(jnp.float32)[None, :, None]
    pieces = []
    for segment in range(segs):
        padded = jnp.pad(gathered[segment], ((0, 0), (0, length)))
        pieces.append(lax.dynamic_slice_in_dim(padded, seg_start[segment], length, axis=1))
    signal = jnp.stack(pieces, axis=0)
    return signal / (window_mean(signal, norm_half) + tiny)


def gathered_plan(raw, alive, seg_start, norm_half):
    segs = raw.shape[0]
    rows = alive.shape[0]
    lag_count = 2 * LAG + 1
    device = lax.axis_index("chan") * lax.axis_size("tm") + lax.axis_index("tm")
    pieces = lax.all_to_all(raw, "tm", split_axis=1, concat_axis=2, tiled=True)
    white = whiten(normalised(pieces, alive, seg_start, norm_half))
    length = white.shape[2]
    everyone = lax.all_gather(white, ("chan", "tm"), axis=1, tiled=True)
    padded = jnp.pad(white, ((0, 0), (0, 0), (LAG, LAG)))
    toeplitz = jnp.stack(
        [padded[:, :, 2 * LAG - lag : 2 * LAG - lag + length] for lag in range(lag_count)], axis=2
    )
    total = jnp.einsum("silt,sjt->ilj", toeplitz, everyone, preferred_element_type=jnp.float32)
    row_ids = device * rows + jnp.arange(rows, dtype=jnp.int32)
    col_ids = jnp.arange(everyone.shape[1], dtype=jnp.int32)
    keep = row_ids[:, None, None] != col_ids[None, None, :]
    scaled = total * (1.0 / math.sqrt(segs * length))
    return jnp.where(keep, scaled, 0.0).astype(jnp.bfloat16)


MESH = pl.DeviceIdType.MESH


def two_parts(table):
    high = table.astype(ml_dtypes.bfloat16)
    low = (table - high.astype(np.float64)).astype(ml_dtypes.bfloat16)
    return np.stack([high, low])


def transform_tables(length):
    half, quarter = length // 2, length // 4
    moments = np.arange(half)
    low_bin, high_bin = length // 250, 2 * length // 5
    ahead, back = [], []
    for parity in range(2):
        bins = 2 * np.arange(quarter) + parity
        angle = 2.0 * np.pi * ((moments[:, None] * bins[None, :]) % length) / length
        ahead.append(np.concatenate([np.cos(angle), -np.sin(angle)], axis=1))
        back.append(np.concatenate([np.cos(angle), -np.sin(angle)], axis=1).T)
    order = np.concatenate([np.arange(0, half, 2), np.arange(1, half, 2)])
    place = np.empty(half, np.int64)
    place[order] = np.arange(half)
    mean = np.zeros((half, half), np.float32)
    for column, bin_index in enumerate(order):
        if low_bin <= bin_index <= high_bin:
            for offset in range(-smooth_half, smooth_half + 1):
                mean[place[abs(bin_index + offset)], column] += 1.0
    return (
        two_parts(np.stack(ahead)),
        two_parts(np.stack(back)),
        mean.astype(ml_dtypes.bfloat16),
    )


def three_parts(value):
    high = value.astype(jnp.bfloat16)
    rest = value - high.astype(jnp.float32)
    middle = rest.astype(jnp.bfloat16)
    low = (rest - middle.astype(jnp.float32)).astype(jnp.bfloat16)
    return jnp.concatenate([high, middle, low], axis=0)


def split_dot(parts, table):
    rows = parts.shape[0] // 3
    result = jnp.dot(parts, table, preferred_element_type=jnp.float32)
    return result[2 * rows :] + result[rows : 2 * rows] + result[:rows]


def table_dot(value, high, low):
    parts = three_parts(value)
    return split_dot(parts, low) + split_dot(parts, high)


def turned(value, by):
    length = value.shape[1]
    return pltpu.roll(value, by % length, 1)


def normed_rows(records, start, alive, half):
    rows, length = records.shape
    signal = records * alive
    bit = 1
    while bit <= length // 4:
        signal = jnp.where((start & bit) != 0, turned(signal, -bit), signal)
        bit *= 2
    lane = lax.broadcasted_iota(jnp.int32, (rows, length), 1)
    signal = jnp.where(lane + start < length, signal, 0.0)
    power = jnp.concatenate([jnp.abs(signal), jnp.zeros((rows, 2 * widest), jnp.float32)], axis=1)
    width = 2 * half + 1
    total = power
    bit = 1
    while bit < 2 * widest:
        power = power + turned(power, -bit)
        bit *= 2
        total = jnp.where((width & bit) != 0, power + turned(total, -bit), total)
    bit = 1
    while bit <= widest:
        total = jnp.where((half & bit) != 0, turned(total, bit), total)
        bit *= 2
    level = total[:, :length] / width.astype(jnp.float32)
    return signal / (level + tiny)


def whiten_rows(normed, ahead, back, mean):
    length = normed.shape[1]
    half, quarter = length // 2, length // 4
    left, right = normed[:, :half], normed[:, half:]
    even = table_dot(left + right, ahead[0, 0], ahead[1, 0])
    odd = table_dot(left - right, ahead[0, 1], ahead[1, 1])
    even_power = even * even
    odd_power = odd * odd
    magnitude = jnp.sqrt(
        jnp.concatenate(
            [
                even_power[:, :quarter] + even_power[:, quarter:],
                odd_power[:, :quarter] + odd_power[:, quarter:],
            ],
            axis=1,
        )
    )
    smooth = split_dot(three_parts(magnitude), mean) / (2 * smooth_half + 1)
    place = lax.broadcasted_iota(jnp.int32, smooth.shape, 1)
    bins = jnp.where(place < quarter, 2 * place, 2 * (place - quarter) + 1)
    keep = (bins >= length // 250) & (bins <= 2 * length // 5)
    gain = jnp.where(keep, 1.0 / (smooth + tiny), 0.0)
    even_gain, odd_gain = gain[:, :quarter], gain[:, quarter:]
    even = even * jnp.concatenate([even_gain, even_gain], axis=1)
    odd = odd * jnp.concatenate([odd_gain, odd_gain], axis=1)
    even = table_dot(even, back[0, 0], back[1, 0])
    odd = table_dot(odd, back[0, 1], back[1, 1])
    return jnp.concatenate([even + odd, even - odd], axis=1) * (2.0 / math.sqrt(length))


def fill_lags(white, target, slot):
    rows, length = white.shape
    ring = jnp.concatenate([white, jnp.zeros((rows, 2 * LAG), jnp.float32)], axis=1)
    ring = turned(ring, -LAG)
    both = jnp.concatenate([ring, turned(ring, 1)], axis=0).astype(jnp.bfloat16)
    for step in range(LAG + 1):
        lagged = turned(both, 2 * step) if step else both
        target[slot, 2 * rows * step : 2 * rows * (step + 1)] = lagged[:, :length]


def fused_kernel(
    raw, alive_hbm, start_hbm, half_hbm, ahead_hbm, back_hbm, mean_hbm, out,
    alive, seg_start, norm_half, small_sem, own_sem, ahead, back, mean, table_sem, records, params, own, other, lagged, totals,
    raw_send, raw_recv, param_send, param_recv, rail_send, rail_recv, core_send, core_recv,
):
    chan, tm = lax.axis_index("chan"), lax.axis_index("tm")
    depth = lax.axis_size("chan") // 2
    groups = lax.axis_size("tm")
    z, y, x, core = chan // 2, chan % 2, tm // 2, tm % 2
    rows = alive.shape[0]
    pair = 2 * rows
    length = own.shape[2]
    blocks = own.shape[0]

    smalls = [
        pltpu.make_async_copy(source, target, small_sem.at[index])
        for index, (source, target) in enumerate(
            [(alive_hbm, alive), (start_hbm, seg_start), (half_hbm, norm_half)]
        )
    ]
    for load in smalls:
        load.start()
    mine_first = pl.multiple_of(x * pair, pair)
    kept = pltpu.make_async_copy(raw.at[core, pl.ds(mine_first, pair)], records.at[tm], own_sem)
    kept.start()
    loads = [
        pltpu.make_async_copy(source, target, table_sem.at[index])
        for index, (source, target) in enumerate(
            [(ahead_hbm, ahead), (mean_hbm, mean), (back_hbm, back)]
        )
    ]
    for load in loads:
        load.start()

    others = [(chan, (tm + step) % groups) for step in range(1, groups)]
    along = [(((z + step) % depth) * 2 + y, tm) for step in range(1, depth)]
    plane = [
        (y, 1 - x),
        (1 - y, x),
        (1 - y, 1 - x),
    ]
    plane_devices = [(z * 2 + py, px * 2 + core) for py, px in plane]
    barrier = pltpu.get_barrier_semaphore()
    greeted = others + along + plane_devices[1:]
    for device in greeted:
        pl.semaphore_signal(barrier, inc=1, device_id=device, device_id_type=MESH)

    for load in smalls:
        load.wait()
    row_ids = lax.broadcasted_iota(jnp.int32, (rows, 128), 0)
    live = jnp.zeros((rows, 128), jnp.int32)
    half = jnp.zeros((rows, 128), jnp.int32)
    for row in range(rows):
        live = jnp.where(row_ids == row, alive[row], live)
        half = jnp.where(row_ids == row, norm_half[row], half)
    params[core] = jnp.concatenate([live, half], axis=0).astype(jnp.float32)
    pl.semaphore_wait(barrier, len(greeted))

    def remote(source, target, send, receive, device):
        return pltpu.make_async_remote_copy(
            src_ref=source, dst_ref=target, send_sem=send, recv_sem=receive,
            device_id=device, device_id_type=MESH,
        )

    started = []
    for step in range(1, groups):
        peer = (tm + step) % groups
        first = pl.multiple_of((peer // 2) * pair, pair)
        copy = remote(
            raw.at[peer % 2, pl.ds(first, pair)], records.at[tm],
            raw_send.at[step - 1], raw_recv.at[tm], (chan, peer),
        )
        copy.start()
        started.append(copy)
    partner = (chan, x * 2 + 1 - core)
    copy = remote(params.at[core], params.at[core], param_send, param_recv, partner)
    copy.start()
    started.append(copy)
    kept.wait()
    for step in range(1, groups):
        peer = (tm + step) % groups
        remote(
            records.at[peer], records.at[peer], raw_send.at[step - 1], raw_recv.at[peer],
            (chan, peer),
        ).wait_recv()
    remote(
        params.at[1 - core], params.at[1 - core], param_send, param_recv, partner
    ).wait_recv()

    gathered = jnp.concatenate([records[group] for group in range(groups)], axis=1)
    live = jnp.concatenate([params[0, :rows], params[1, :rows]], axis=0)[:, :1]
    half = jnp.concatenate([params[0, rows:], params[1, rows:]], axis=0)[:, :1]
    normed = normed_rows(gathered, seg_start[core], live, half.astype(jnp.int32))
    for load in loads:
        load.wait()
    white = whiten_rows(normed, ahead, back, mean[...]).astype(jnp.bfloat16)

    def block_of(bz, by, bx):
        return (bz * 2 + by) * 2 + bx

    def to_core(block):
        copy = remote(
            own.at[block], other.at[block], core_send.at[block], core_recv.at[block], partner
        )
        copy.start()
        started.append(copy)

    def to_side(block, side, semaphore):
        copy = remote(
            own.at[block], own.at[block], semaphore, rail_recv.at[block], plane_devices[side]
        )
        copy.start()
        started.append(copy)

    def to_plane(block, step):
        for side in range(2):
            to_side(block, side, rail_send.at[step, side])

    def arrived(buffer, semaphores, block):
        remote(
            buffer.at[block], buffer.at[block], core_send.at[block], semaphores.at[block], partner
        ).wait_recv()

    mine = block_of(z, y, x)
    own[mine] = white
    for index, device in enumerate(along):
        copy = remote(
            own.at[mine], own.at[mine], rail_send.at[depth, index], rail_recv.at[mine], device
        )
        copy.start()
        started.append(copy)
    to_plane(mine, 0)
    to_core(mine)

    wide = white.astype(jnp.float32)
    fill_lags(jnp.where(core == 0, wide[:rows], wide[rows:]), lagged, 0)

    for step in range(1, depth):
        block = block_of((z + step) % depth, y, x)
        arrived(own, rail_recv, block)
        to_plane(block, step)
        to_core(block)

    arrived(other, core_recv, mine)
    wide = other[mine].astype(jnp.float32)
    fill_lags(jnp.where(core == 0, wide[:rows], wide[rows:]), lagged, 1)

    for step in range(depth):
        for side in range(2):
            block = block_of((z + step) % depth, *plane[side])
            arrived(own, rail_recv, block)
            if step % 2 == side:
                to_side(block, 1 - side, rail_send.at[step, 2])
            to_core(block)
    for step in range(depth):
        block = block_of((z + step) % depth, *plane[2])
        arrived(own, rail_recv, block)
        to_core(block)

    def lag_dot(slot, columns):
        return lax.dot_general(
            lagged[slot],
            columns[...].reshape(blocks * pair, length),
            (((1,), (1,)), ((), ())),
            preferred_element_type=jnp.float32,
        )

    totals[...] = lag_dot(0, own)
    for step in range(depth):
        for py, px in [(y, x)] + plane:
            if step == 0 and px is x and py is y:
                continue
            arrived(other, core_recv, block_of((z + step) % depth, py, px))
    lag_count = out.shape[0]
    shape = (lag_count * rows, blocks * pair)
    ahead_by = lax.broadcasted_iota(jnp.int32, shape, 1) - (chan * groups + tm) * rows
    same = ahead_by == lax.broadcasted_iota(jnp.int32, shape, 0) % rows
    result = (totals[...] + lag_dot(1, other))[: lag_count * rows]
    result = jnp.where(same, 0.0, result * (1.0 / math.sqrt(2 * length)))
    out[...] = result.reshape(out.shape).astype(jnp.bfloat16)
    for copy in started:
        copy.wait_send()


def fused_plan(raw, alive, seg_start, norm_half):
    segs, width, span = raw.shape
    groups, chans = lax.axis_size("tm"), lax.axis_size("chan")
    rows = alive.shape[0]
    length = span * groups
    depth = chans // 2
    blocks = chans * 2
    half = length // 2
    lag_rows = 2 * (LAG + 1) * rows
    ahead, back, mean = transform_tables(length)
    vmem = pl.BlockSpec(memory_space=pltpu.VMEM)
    hbm = pl.BlockSpec(memory_space=pltpu.HBM)
    dma = pltpu.SemaphoreType.DMA
    corr = pl.pallas_call(
        fused_kernel,
        out_shape=jax.ShapeDtypeStruct((2 * LAG + 1, rows, width * chans), jnp.bfloat16),
        in_specs=[hbm] * 7,
        out_specs=vmem,
        scratch_shapes=[
            pltpu.SMEM((rows,), jnp.int32),
            pltpu.SMEM((segs,), jnp.int32),
            pltpu.SMEM((rows,), jnp.int32),
            dma((3,)),
            dma(()),
            pltpu.VMEM((2, 2, half, half), jnp.bfloat16),
            pltpu.VMEM((2, 2, half, half), jnp.bfloat16),
            pltpu.VMEM((half, half), jnp.bfloat16),
            dma((3,)),
            pltpu.VMEM((groups, 2 * rows, span), jnp.float32),
            pltpu.VMEM((2, 2 * rows, 128), jnp.float32),
            pltpu.VMEM((blocks, 2 * rows, length), jnp.bfloat16),
            pltpu.VMEM((blocks, 2 * rows, length), jnp.bfloat16),
            pltpu.VMEM((2, lag_rows, length), jnp.bfloat16),
            pltpu.VMEM((lag_rows, width * chans), jnp.float32),
            dma((groups - 1,)),
            dma((groups,)),
            dma(()),
            dma(()),
            dma((depth + 1, 3)),
            dma((blocks,)),
            dma((blocks,)),
            dma((blocks,)),
        ],
        compiler_params=pltpu.CompilerParams(
            collective_id=0, has_side_effects=True, vmem_limit_bytes=60 * 1024 * 1024
        ),
        cost_estimate=pl.CostEstimate(
            flops=4 * lag_rows * length * width * chans,
            bytes_accessed=6 * 1024 * 1024,
            transcendentals=0,
        ),
    )(raw, alive, seg_start, norm_half, ahead, back, mean)
    return jnp.transpose(corr, (1, 0, 2))


def on_device(raw, alive, seg_start, norm_half):
    segs, width, span = raw.shape
    shape = (lax.axis_size("chan"), lax.axis_size("tm"), segs, alive.shape[0], span)
    if shape == (8, 4, 2, 8, 256):
        return fused_plan(raw, alive, seg_start, norm_half)
    return gathered_plan(raw, alive, seg_start, norm_half)


def solution(mesh):
    return jax.shard_map(
        on_device,
        mesh=mesh,
        in_specs=(P(None, "chan", "tm"), P(("chan", "tm")), P(), P(("chan", "tm"))),
        out_specs=P(("chan", "tm"), None, None),
        check_vma=False,
    )
```

```python
import math

import jax
import jax.numpy as jnp
import ml_dtypes
import numpy as np
from jax import lax
from jax.experimental import pallas as pl
from jax.experimental.pallas import tpu as pltpu
from jax.sharding import PartitionSpec as P

LAG = 64


widest = 64
smooth_half = 32
tiny = 1e-05
radix = 128


def window_mean(signal, half_width):
    length = signal.shape[2]
    half = half_width[None, :, None]
    width = 2 * half + 1
    power = jnp.pad(jnp.abs(signal), ((0, 0), (0, 0), (widest, widest)))

    def ahead(value, by):
        return jnp.pad(value[:, :, by:], ((0, 0), (0, 0), (0, by)))

    total = jnp.zeros_like(power)
    span = 1
    while span <= 2 * widest + 1:
        total = jnp.where((width & span) != 0, power + ahead(total, span), total)
        power = power + ahead(power, span)
        span *= 2
    rest = widest - half
    span = 1
    while span <= widest:
        total = jnp.where((rest & span) != 0, ahead(total, span), total)
        span *= 2
    return total[:, :, :length] / width.astype(jnp.float32)


def phase_table(row_total, col_total, modulus):
    product = (
        jnp.arange(row_total, dtype=jnp.int32)[:, None]
        * jnp.arange(col_total, dtype=jnp.int32)[None, :]
        % modulus
    )
    angle = product.astype(jnp.float32) * (2.0 * math.pi / modulus)
    return (jnp.cos(angle), jnp.sin(angle))


def forward_transform(signal, cos_q, sin_q, cos_p, sin_p, cos_t, sin_t):
    length = signal.shape[1]
    inner = length // radix
    highest = lax.Precision.HIGHEST
    grid = signal.reshape(-1, inner, radix)
    first_re = jnp.einsum("rqp,qk->rkp", grid, cos_q, precision=highest)
    first_im = -jnp.einsum("rqp,qk->rkp", grid, sin_q, precision=highest)
    turned_re = first_re * cos_t + first_im * sin_t
    turned_im = first_im * cos_t - first_re * sin_t
    out_re = jnp.einsum("rkp,pj->rjk", turned_re, cos_p, precision=highest) + jnp.einsum(
        "rkp,pj->rjk", turned_im, sin_p, precision=highest
    )
    out_im = jnp.einsum("rkp,pj->rjk", turned_im, cos_p, precision=highest) - jnp.einsum(
        "rkp,pj->rjk", turned_re, sin_p, precision=highest
    )
    return (out_re.reshape(-1, length), out_im.reshape(-1, length))


def inverse_real(spec_re, spec_im, cos_q, sin_q, cos_p, sin_p, cos_t, sin_t):
    length = spec_re.shape[1]
    inner = length // radix
    highest = lax.Precision.HIGHEST
    grid_re = spec_re.reshape(-1, radix, inner)
    grid_im = spec_im.reshape(-1, radix, inner)
    first_re = jnp.einsum("rjk,jp->rkp", grid_re, cos_p, precision=highest) - jnp.einsum(
        "rjk,jp->rkp", grid_im, sin_p, precision=highest
    )
    first_im = jnp.einsum("rjk,jp->rkp", grid_im, cos_p, precision=highest) + jnp.einsum(
        "rjk,jp->rkp", grid_re, sin_p, precision=highest
    )
    turned_re = first_re * cos_t - first_im * sin_t
    turned_im = first_im * cos_t + first_re * sin_t
    result = jnp.einsum("rkp,kq->rqp", turned_re, cos_q, precision=highest) - jnp.einsum(
        "rkp,kq->rqp", turned_im, sin_q, precision=highest
    )
    return result.reshape(-1, length)


def whiten(normed):
    segs, rows, length = normed.shape
    inner = length // radix
    cos_q, sin_q = phase_table(inner, inner, inner)
    cos_p, sin_p = phase_table(radix, radix, radix)
    cos_t, sin_t = phase_table(inner, radix, length)
    spec_re, spec_im = forward_transform(
        normed.reshape(-1, length), cos_q, sin_q, cos_p, sin_p, cos_t, sin_t
    )
    magnitude = jnp.sqrt(spec_re * spec_re + spec_im * spec_im)
    circular = jnp.concatenate(
        [magnitude[:, length - smooth_half :], magnitude, magnitude[:, :smooth_half]], axis=1
    )
    running = jnp.cumsum(circular, axis=1)
    running = jnp.concatenate([jnp.zeros((running.shape[0], 1), jnp.float32), running], axis=1)
    span_bins = 2 * smooth_half + 1
    smooth = (running[:, span_bins:] - running[:, :-span_bins]) / span_bins
    bins = jnp.arange(length, dtype=jnp.int32)
    folded = jnp.minimum(bins, length - bins)
    band = ((folded >= length // 250) & (folded <= 2 * length // 5)).astype(jnp.float32)
    gain = band[None, :] / (smooth + tiny)
    traces = inverse_real(spec_re * gain, spec_im * gain, cos_q, sin_q, cos_p, sin_p, cos_t, sin_t)
    return (traces * (1.0 / math.sqrt(length))).reshape(segs, rows, length).astype(jnp.bfloat16)


def normalised(gathered, alive, seg_start, norm_half):
    segs, rows, length = gathered.shape
    gathered = gathered * alive.astype(jnp.float32)[None, :, None]
    pieces = []
    for segment in range(segs):
        padded = jnp.pad(gathered[segment], ((0, 0), (0, length)))
        pieces.append(lax.dynamic_slice_in_dim(padded, seg_start[segment], length, axis=1))
    signal = jnp.stack(pieces, axis=0)
    return signal / (window_mean(signal, norm_half) + tiny)


def gathered_plan(raw, alive, seg_start, norm_half):
    segs = raw.shape[0]
    rows = alive.shape[0]
    lag_count = 2 * LAG + 1
    device = lax.axis_index("chan") * lax.axis_size("tm") + lax.axis_index("tm")
    pieces = lax.all_to_all(raw, "tm", split_axis=1, concat_axis=2, tiled=True)
    white = whiten(normalised(pieces, alive, seg_start, norm_half))
    length = white.shape[2]
    everyone = lax.all_gather(white, ("chan", "tm"), axis=1, tiled=True)
    padded = jnp.pad(white, ((0, 0), (0, 0), (LAG, LAG)))
    toeplitz = jnp.stack(
        [padded[:, :, 2 * LAG - lag : 2 * LAG - lag + length] for lag in range(lag_count)], axis=2
    )
    total = jnp.einsum("silt,sjt->ilj", toeplitz, everyone, preferred_element_type=jnp.float32)
    row_ids = device * rows + jnp.arange(rows, dtype=jnp.int32)
    col_ids = jnp.arange(everyone.shape[1], dtype=jnp.int32)
    keep = row_ids[:, None, None] != col_ids[None, None, :]
    scaled = total * (1.0 / math.sqrt(segs * length))
    return jnp.where(keep, scaled, 0.0).astype(jnp.bfloat16)


MESH = pl.DeviceIdType.MESH


def two_parts(table):
    high = table.astype(ml_dtypes.bfloat16)
    low = (table - high.astype(np.float64)).astype(ml_dtypes.bfloat16)
    return np.stack([high, low])


def transform_tables(length):
    half, quarter = length // 2, length // 4
    moments = np.arange(half)
    low_bin, high_bin = length // 250, 2 * length // 5
    ahead, back = [], []
    for parity in range(2):
        bins = 2 * np.arange(quarter) + parity
        angle = 2.0 * np.pi * ((moments[:, None] * bins[None, :]) % length) / length
        ahead.append(np.concatenate([np.cos(angle), -np.sin(angle)], axis=1))
        back.append(np.concatenate([np.cos(angle), -np.sin(angle)], axis=1).T)
    order = np.concatenate([np.arange(0, half, 2), np.arange(1, half, 2)])
    place = np.empty(half, np.int64)
    place[order] = np.arange(half)
    mean = np.zeros((half, half), np.float32)
    for column, bin_index in enumerate(order):
        if low_bin <= bin_index <= high_bin:
            for offset in range(-smooth_half, smooth_half + 1):
                mean[place[abs(bin_index + offset)], column] += 1.0
    return (
        two_parts(np.stack(ahead)),
        two_parts(np.stack(back)),
        mean.astype(ml_dtypes.bfloat16),
    )


def three_parts(value):
    high = value.astype(jnp.bfloat16)
    rest = value - high.astype(jnp.float32)
    middle = rest.astype(jnp.bfloat16)
    low = (rest - middle.astype(jnp.float32)).astype(jnp.bfloat16)
    return jnp.concatenate([high, middle, low], axis=0)


def split_dot(parts, table):
    rows = parts.shape[0] // 3
    result = jnp.dot(parts, table, preferred_element_type=jnp.float32)
    return result[2 * rows :] + result[rows : 2 * rows] + result[:rows]


def table_dot(value, high, low):
    parts = three_parts(value)
    return split_dot(parts, low) + split_dot(parts, high)


def turned(value, by):
    length = value.shape[1]
    return pltpu.roll(value, by % length, 1)


def normed_rows(records, start, alive, half):
    rows, length = records.shape
    signal = records * alive
    bit = 1
    while bit <= length // 4:
        signal = jnp.where((start & bit) != 0, turned(signal, -bit), signal)
        bit *= 2
    lane = lax.broadcasted_iota(jnp.int32, (rows, length), 1)
    signal = jnp.where(lane + start < length, signal, 0.0)
    power = jnp.concatenate([jnp.abs(signal), jnp.zeros((rows, 2 * widest), jnp.float32)], axis=1)
    width = 2 * half + 1
    total = power
    bit = 1
    while bit < 2 * widest:
        power = power + turned(power, -bit)
        bit *= 2
        total = jnp.where((width & bit) != 0, power + turned(total, -bit), total)
    bit = 1
    while bit <= widest:
        total = jnp.where((half & bit) != 0, turned(total, bit), total)
        bit *= 2
    level = total[:, :length] / width.astype(jnp.float32)
    return signal / (level + tiny)


def whiten_rows(normed, ahead, back, mean):
    length = normed.shape[1]
    half, quarter = length // 2, length // 4
    left, right = normed[:, :half], normed[:, half:]
    even = table_dot(left + right, ahead[0, 0], ahead[1, 0])
    odd = table_dot(left - right, ahead[0, 1], ahead[1, 1])
    even_power = even * even
    odd_power = odd * odd
    magnitude = jnp.sqrt(
        jnp.concatenate(
            [
                even_power[:, :quarter] + even_power[:, quarter:],
                odd_power[:, :quarter] + odd_power[:, quarter:],
            ],
            axis=1,
        )
    )
    smooth = split_dot(three_parts(magnitude), mean) / (2 * smooth_half + 1)
    place = lax.broadcasted_iota(jnp.int32, smooth.shape, 1)
    bins = jnp.where(place < quarter, 2 * place, 2 * (place - quarter) + 1)
    keep = (bins >= length // 250) & (bins <= 2 * length // 5)
    gain = jnp.where(keep, 1.0 / (smooth + tiny), 0.0)
    even_gain, odd_gain = gain[:, :quarter], gain[:, quarter:]
    even = even * jnp.concatenate([even_gain, even_gain], axis=1)
    odd = odd * jnp.concatenate([odd_gain, odd_gain], axis=1)
    even = table_dot(even, back[0, 0], back[1, 0])
    odd = table_dot(odd, back[0, 1], back[1, 1])
    return jnp.concatenate([even + odd, even - odd], axis=1) * (2.0 / math.sqrt(length))


def fill_lags(white, target, slot):
    rows, length = white.shape
    ring = jnp.concatenate([white, jnp.zeros((rows, 2 * LAG), jnp.float32)], axis=1)
    ring = turned(ring, -LAG)
    both = jnp.concatenate([ring, turned(ring, 1)], axis=0).astype(jnp.bfloat16)
    for step in range(LAG + 1):
        lagged = turned(both, 2 * step) if step else both
        target[slot, 2 * rows * step : 2 * rows * (step + 1)] = lagged[:, :length]


def fused_kernel(
    raw, alive_hbm, start_hbm, half_hbm, ahead_hbm, back_hbm, mean_hbm, out,
    alive, seg_start, norm_half, small_sem, own_sem, ahead, back, mean, table_sem, records, params, own, other, lagged, totals,
    raw_send, raw_recv, param_send, param_recv, rail_send, rail_recv, core_send, core_recv,
):
    chan, tm = lax.axis_index("chan"), lax.axis_index("tm")
    depth = lax.axis_size("chan") // 2
    groups = lax.axis_size("tm")
    z, y, x, core = chan // 2, chan % 2, tm // 2, tm % 2
    rows = alive.shape[0]
    pair = 2 * rows
    length = own.shape[2]
    blocks = own.shape[0]

    smalls = [
        pltpu.make_async_copy(source, target, small_sem.at[index])
        for index, (source, target) in enumerate(
            [(alive_hbm, alive), (start_hbm, seg_start), (half_hbm, norm_half)]
        )
    ]
    for load in smalls:
        load.start()
    mine_first = pl.multiple_of(x * pair, pair)
    kept = pltpu.make_async_copy(raw.at[core, pl.ds(mine_first, pair)], records.at[tm], own_sem)
    kept.start()
    loads = [
        pltpu.make_async_copy(source, target, table_sem.at[index])
        for index, (source, target) in enumerate(
            [(ahead_hbm, ahead), (mean_hbm, mean), (back_hbm, back)]
        )
    ]
    for load in loads[:2]:
        load.start()

    near = [z, z + 1 - 2 * (z % 2), z + 2 - 4 * (z // 2), 3 - z]
    others = [(chan, (tm + step) % groups) for step in range(1, groups)]
    along = [(level * 2 + y, tm) for level in near[1:]]
    plane = [
        (y, 1 - x),
        (1 - y, x),
        (1 - y, 1 - x),
    ]
    plane_devices = [(z * 2 + py, px * 2 + core) for py, px in plane]
    barrier = pltpu.get_barrier_semaphore()
    greeted = others + along + plane_devices[1:]
    for device in greeted:
        pl.semaphore_signal(barrier, inc=1, device_id=device, device_id_type=MESH)

    for load in smalls:
        load.wait()
    row_ids = lax.broadcasted_iota(jnp.int32, (rows, 128), 0)
    live = jnp.zeros((rows, 128), jnp.int32)
    half = jnp.zeros((rows, 128), jnp.int32)
    for row in range(rows):
        live = jnp.where(row_ids == row, alive[row], live)
        half = jnp.where(row_ids == row, norm_half[row], half)
    params[core] = jnp.concatenate([live, half], axis=0).astype(jnp.float32)
    pl.semaphore_wait(barrier, len(greeted))

    def remote(source, target, send, receive, device):
        return pltpu.make_async_remote_copy(
            src_ref=source, dst_ref=target, send_sem=send, recv_sem=receive,
            device_id=device, device_id_type=MESH,
        )

    started = []
    for step in range(1, groups):
        peer = (tm + step) % groups
        first = pl.multiple_of((peer // 2) * pair, pair)
        copy = remote(
            raw.at[peer % 2, pl.ds(first, pair)], records.at[tm],
            raw_send.at[step - 1], raw_recv.at[tm], (chan, peer),
        )
        copy.start()
        started.append(copy)
    loads[2].start()
    partner = (chan, x * 2 + 1 - core)
    copy = remote(params.at[core], params.at[core], param_send, param_recv, partner)
    copy.start()
    started.append(copy)
    kept.wait()
    for step in range(1, groups):
        peer = (tm + step) % groups
        remote(
            records.at[peer], records.at[peer], raw_send.at[step - 1], raw_recv.at[peer],
            (chan, peer),
        ).wait_recv()
    remote(
        params.at[1 - core], params.at[1 - core], param_send, param_recv, partner
    ).wait_recv()

    gathered = jnp.concatenate([records[group] for group in range(groups)], axis=1)
    live = jnp.concatenate([params[0, :rows], params[1, :rows]], axis=0)[:, :1]
    half = jnp.concatenate([params[0, rows:], params[1, rows:]], axis=0)[:, :1]
    normed = normed_rows(gathered, seg_start[core], live, half.astype(jnp.int32))
    for load in loads:
        load.wait()
    white = whiten_rows(normed, ahead, back, mean[...]).astype(jnp.bfloat16)

    def block_of(bz, by, bx):
        return (bz * 2 + by) * 2 + bx

    def to_core(block):
        copy = remote(
            own.at[block], other.at[block], core_send.at[block], core_recv.at[block], partner
        )
        copy.start()
        started.append(copy)

    def to_side(block, side, semaphore):
        copy = remote(
            own.at[block], own.at[block], semaphore, rail_recv.at[block], plane_devices[side]
        )
        copy.start()
        started.append(copy)

    def to_plane(block, step):
        for side in range(2):
            to_side(block, side, rail_send.at[step, side])

    def arrived(buffer, semaphores, block):
        remote(
            buffer.at[block], buffer.at[block], core_send.at[block], semaphores.at[block], partner
        ).wait_recv()

    mine = block_of(z, y, x)
    own[mine] = white
    for index, device in enumerate(along):
        copy = remote(
            own.at[mine], own.at[mine], rail_send.at[depth, index], rail_recv.at[mine], device
        )
        copy.start()
        started.append(copy)
    to_plane(mine, 0)
    to_core(mine)

    wide = white.astype(jnp.float32)
    fill_lags(jnp.where(core == 0, wide[:rows], wide[rows:]), lagged, 0)

    for step in range(1, depth):
        block = block_of(near[step], y, x)
        arrived(own, rail_recv, block)
        to_plane(block, step)
        to_core(block)

    arrived(other, core_recv, mine)
    wide = other[mine].astype(jnp.float32)
    fill_lags(jnp.where(core == 0, wide[:rows], wide[rows:]), lagged, 1)

    for step in range(depth):
        for side in range(2):
            block = block_of(near[step], *plane[side])
            arrived(own, rail_recv, block)
            if step % 2 == side:
                to_side(block, 1 - side, rail_send.at[step, 2])
            to_core(block)
    for step in range(depth):
        block = block_of(near[step], *plane[2])
        arrived(own, rail_recv, block)
        to_core(block)

    def lag_dot(slot, columns):
        return lax.dot_general(
            lagged[slot],
            columns[...].reshape(blocks * pair, length),
            (((1,), (1,)), ((), ())),
            preferred_element_type=jnp.float32,
        )

    totals[...] = lag_dot(0, own)
    for step in range(depth):
        for py, px in [(y, x)] + plane:
            if step == 0 and px is x and py is y:
                continue
            arrived(other, core_recv, block_of(near[step], py, px))
    lag_count = out.shape[0]
    shape = (rows, blocks * pair)
    ahead_by = lax.broadcasted_iota(jnp.int32, shape, 1) - (chan * groups + tm) * rows
    same = ahead_by == lax.broadcasted_iota(jnp.int32, shape, 0)
    result = (totals[...] + lag_dot(1, other))[: lag_count * rows].reshape(out.shape)
    result = jnp.where(same[None], 0.0, result * (1.0 / math.sqrt(2 * length)))
    out[...] = result.astype(jnp.bfloat16)
    for copy in started:
        copy.wait_send()


def fused_plan(raw, alive, seg_start, norm_half):
    segs, width, span = raw.shape
    groups, chans = lax.axis_size("tm"), lax.axis_size("chan")
    rows = alive.shape[0]
    length = span * groups
    depth = chans // 2
    blocks = chans * 2
    half = length // 2
    lag_rows = 2 * (LAG + 1) * rows
    ahead, back, mean = transform_tables(length)
    operands = (raw, alive, seg_start, norm_half, ahead, back, mean)
    operands = [jnp.asarray(operand) for operand in operands]
    vmem = pl.BlockSpec(memory_space=pltpu.VMEM)
    hbm = pl.BlockSpec(memory_space=pltpu.HBM)
    dma = pltpu.SemaphoreType.DMA
    corr = pl.pallas_call(
        fused_kernel,
        out_shape=pltpu.VMEM((2 * LAG + 1, rows, width * chans), jnp.bfloat16),
        in_specs=[hbm] * 7,
        out_specs=vmem,
        scratch_shapes=[
            pltpu.SMEM((rows,), jnp.int32),
            pltpu.SMEM((segs,), jnp.int32),
            pltpu.SMEM((rows,), jnp.int32),
            dma((3,)),
            dma(()),
            pltpu.VMEM((2, 2, half, half), jnp.bfloat16),
            pltpu.VMEM((2, 2, half, half), jnp.bfloat16),
            pltpu.VMEM((half, half), jnp.bfloat16),
            dma((3,)),
            pltpu.VMEM((groups, 2 * rows, span), jnp.float32),
            pltpu.VMEM((2, 2 * rows, 128), jnp.float32),
            pltpu.VMEM((blocks, 2 * rows, length), jnp.bfloat16),
            pltpu.VMEM((blocks, 2 * rows, length), jnp.bfloat16),
            pltpu.VMEM((2, lag_rows, length), jnp.bfloat16),
            pltpu.VMEM((lag_rows, width * chans), jnp.float32),
            dma((groups - 1,)),
            dma((groups,)),
            dma(()),
            dma(()),
            dma((depth + 1, 3)),
            dma((blocks,)),
            dma((blocks,)),
            dma((blocks,)),
        ],
        compiler_params=pltpu.CompilerParams(
            collective_id=0, has_side_effects=True, vmem_limit_bytes=48 * 1024 * 1024
        ),
        cost_estimate=pl.CostEstimate(
            flops=4 * lag_rows * length * width * chans,
            bytes_accessed=6 * 1024 * 1024,
            transcendentals=0,
        ),
    )(*[pltpu.with_memory_space_constraint(operand, pltpu.HBM) for operand in operands])
    return jnp.transpose(corr, (1, 0, 2))


def on_device(raw, alive, seg_start, norm_half):
    segs, width, span = raw.shape
    shape = (lax.axis_size("chan"), lax.axis_size("tm"), segs, alive.shape[0], span)
    if shape == (8, 4, 2, 8, 256):
        return fused_plan(raw, alive, seg_start, norm_half)
    return gathered_plan(raw, alive, seg_start, norm_half)


def solution(mesh):
    return jax.shard_map(
        on_device,
        mesh=mesh,
        in_specs=(P(None, "chan", "tm"), P(("chan", "tm")), P(), P(("chan", "tm"))),
        out_specs=P(("chan", "tm"), None, None),
        check_vma=False,
    )
```

```python
import math

import jax
import jax.numpy as jnp
import ml_dtypes
import numpy as np
from jax import lax
from jax.experimental import pallas as pl
from jax.experimental.pallas import tpu as pltpu
from jax.sharding import PartitionSpec as P

LAG = 64


widest = 64
smooth_half = 32
tiny = 1e-05
radix = 128


def window_mean(signal, half_width):
    length = signal.shape[2]
    half = half_width[None, :, None]
    width = 2 * half + 1
    power = jnp.pad(jnp.abs(signal), ((0, 0), (0, 0), (widest, widest)))

    def ahead(value, by):
        return jnp.pad(value[:, :, by:], ((0, 0), (0, 0), (0, by)))

    total = jnp.zeros_like(power)
    span = 1
    while span <= 2 * widest + 1:
        total = jnp.where((width & span) != 0, power + ahead(total, span), total)
        power = power + ahead(power, span)
        span *= 2
    rest = widest - half
    span = 1
    while span <= widest:
        total = jnp.where((rest & span) != 0, ahead(total, span), total)
        span *= 2
    return total[:, :, :length] / width.astype(jnp.float32)


def phase_table(row_total, col_total, modulus):
    product = (
        jnp.arange(row_total, dtype=jnp.int32)[:, None]
        * jnp.arange(col_total, dtype=jnp.int32)[None, :]
        % modulus
    )
    angle = product.astype(jnp.float32) * (2.0 * math.pi / modulus)
    return (jnp.cos(angle), jnp.sin(angle))


def forward_transform(signal, cos_q, sin_q, cos_p, sin_p, cos_t, sin_t):
    length = signal.shape[1]
    inner = length // radix
    highest = lax.Precision.HIGHEST
    grid = signal.reshape(-1, inner, radix)
    first_re = jnp.einsum("rqp,qk->rkp", grid, cos_q, precision=highest)
    first_im = -jnp.einsum("rqp,qk->rkp", grid, sin_q, precision=highest)
    turned_re = first_re * cos_t + first_im * sin_t
    turned_im = first_im * cos_t - first_re * sin_t
    out_re = jnp.einsum("rkp,pj->rjk", turned_re, cos_p, precision=highest) + jnp.einsum(
        "rkp,pj->rjk", turned_im, sin_p, precision=highest
    )
    out_im = jnp.einsum("rkp,pj->rjk", turned_im, cos_p, precision=highest) - jnp.einsum(
        "rkp,pj->rjk", turned_re, sin_p, precision=highest
    )
    return (out_re.reshape(-1, length), out_im.reshape(-1, length))


def inverse_real(spec_re, spec_im, cos_q, sin_q, cos_p, sin_p, cos_t, sin_t):
    length = spec_re.shape[1]
    inner = length // radix
    highest = lax.Precision.HIGHEST
    grid_re = spec_re.reshape(-1, radix, inner)
    grid_im = spec_im.reshape(-1, radix, inner)
    first_re = jnp.einsum("rjk,jp->rkp", grid_re, cos_p, precision=highest) - jnp.einsum(
        "rjk,jp->rkp", grid_im, sin_p, precision=highest
    )
    first_im = jnp.einsum("rjk,jp->rkp", grid_im, cos_p, precision=highest) + jnp.einsum(
        "rjk,jp->rkp", grid_re, sin_p, precision=highest
    )
    turned_re = first_re * cos_t - first_im * sin_t
    turned_im = first_im * cos_t + first_re * sin_t
    result = jnp.einsum("rkp,kq->rqp", turned_re, cos_q, precision=highest) - jnp.einsum(
        "rkp,kq->rqp", turned_im, sin_q, precision=highest
    )
    return result.reshape(-1, length)


def whiten(normed):
    segs, rows, length = normed.shape
    inner = length // radix
    cos_q, sin_q = phase_table(inner, inner, inner)
    cos_p, sin_p = phase_table(radix, radix, radix)
    cos_t, sin_t = phase_table(inner, radix, length)
    spec_re, spec_im = forward_transform(
        normed.reshape(-1, length), cos_q, sin_q, cos_p, sin_p, cos_t, sin_t
    )
    magnitude = jnp.sqrt(spec_re * spec_re + spec_im * spec_im)
    circular = jnp.concatenate(
        [magnitude[:, length - smooth_half :], magnitude, magnitude[:, :smooth_half]], axis=1
    )
    running = jnp.cumsum(circular, axis=1)
    running = jnp.concatenate([jnp.zeros((running.shape[0], 1), jnp.float32), running], axis=1)
    span_bins = 2 * smooth_half + 1
    smooth = (running[:, span_bins:] - running[:, :-span_bins]) / span_bins
    bins = jnp.arange(length, dtype=jnp.int32)
    folded = jnp.minimum(bins, length - bins)
    band = ((folded >= length // 250) & (folded <= 2 * length // 5)).astype(jnp.float32)
    gain = band[None, :] / (smooth + tiny)
    traces = inverse_real(spec_re * gain, spec_im * gain, cos_q, sin_q, cos_p, sin_p, cos_t, sin_t)
    return (traces * (1.0 / math.sqrt(length))).reshape(segs, rows, length).astype(jnp.bfloat16)


def normalised(gathered, alive, seg_start, norm_half):
    segs, rows, length = gathered.shape
    gathered = gathered * alive.astype(jnp.float32)[None, :, None]
    pieces = []
    for segment in range(segs):
        padded = jnp.pad(gathered[segment], ((0, 0), (0, length)))
        pieces.append(lax.dynamic_slice_in_dim(padded, seg_start[segment], length, axis=1))
    signal = jnp.stack(pieces, axis=0)
    return signal / (window_mean(signal, norm_half) + tiny)


def gathered_plan(raw, alive, seg_start, norm_half):
    segs = raw.shape[0]
    rows = alive.shape[0]
    lag_count = 2 * LAG + 1
    device = lax.axis_index("chan") * lax.axis_size("tm") + lax.axis_index("tm")
    pieces = lax.all_to_all(raw, "tm", split_axis=1, concat_axis=2, tiled=True)
    white = whiten(normalised(pieces, alive, seg_start, norm_half))
    length = white.shape[2]
    everyone = lax.all_gather(white, ("chan", "tm"), axis=1, tiled=True)
    padded = jnp.pad(white, ((0, 0), (0, 0), (LAG, LAG)))
    toeplitz = jnp.stack(
        [padded[:, :, 2 * LAG - lag : 2 * LAG - lag + length] for lag in range(lag_count)], axis=2
    )
    total = jnp.einsum("silt,sjt->ilj", toeplitz, everyone, preferred_element_type=jnp.float32)
    row_ids = device * rows + jnp.arange(rows, dtype=jnp.int32)
    col_ids = jnp.arange(everyone.shape[1], dtype=jnp.int32)
    keep = row_ids[:, None, None] != col_ids[None, None, :]
    scaled = total * (1.0 / math.sqrt(segs * length))
    return jnp.where(keep, scaled, 0.0).astype(jnp.bfloat16)


MESH = pl.DeviceIdType.MESH


def two_parts(table):
    high = table.astype(ml_dtypes.bfloat16)
    low = (table - high.astype(np.float64)).astype(ml_dtypes.bfloat16)
    return np.stack([high, low])


def transform_tables(length):
    half, quarter = length // 2, length // 4
    moments = np.arange(half)
    low_bin, high_bin = length // 250, 2 * length // 5
    ahead, back = [], []
    for parity in range(2):
        bins = 2 * np.arange(quarter) + parity
        angle = 2.0 * np.pi * ((moments[:, None] * bins[None, :]) % length) / length
        ahead.append(np.concatenate([np.cos(angle), -np.sin(angle)], axis=1))
        back.append(np.concatenate([np.cos(angle), -np.sin(angle)], axis=1).T)
    order = np.concatenate([np.arange(0, half, 2), np.arange(1, half, 2)])
    place = np.empty(half, np.int64)
    place[order] = np.arange(half)
    mean = np.zeros((half, half), np.float32)
    for column, bin_index in enumerate(order):
        if low_bin <= bin_index <= high_bin:
            for offset in range(-smooth_half, smooth_half + 1):
                mean[place[abs(bin_index + offset)], column] += 1.0
    return (
        two_parts(np.stack(ahead)),
        two_parts(np.stack(back)),
        mean.astype(ml_dtypes.bfloat16),
    )


def three_parts(value):
    high = value.astype(jnp.bfloat16)
    rest = value - high.astype(jnp.float32)
    middle = rest.astype(jnp.bfloat16)
    low = (rest - middle.astype(jnp.float32)).astype(jnp.bfloat16)
    return jnp.concatenate([high, middle, low], axis=0)


def split_dot(parts, table):
    rows = parts.shape[0] // 3
    result = jnp.dot(parts, table, preferred_element_type=jnp.float32)
    return result[2 * rows :] + result[rows : 2 * rows] + result[:rows]


def table_dot(value, high, low):
    parts = three_parts(value)
    return split_dot(parts, low) + split_dot(parts, high)


def turned(value, by):
    length = value.shape[1]
    return pltpu.roll(value, by % length, 1)


def window_sum(first, count, limit, way):
    power = first
    total = jnp.where((count & 1) != 0, power, 0.0)
    bit = 1
    while 2 * bit <= limit:
        power = power + turned(power, way * bit)
        bit *= 2
        total = jnp.where((count & bit) != 0, power + turned(total, way * bit), total)
    return total


def normed_rows(records, start, alive, half):
    rows, length = records.shape
    signal = records * jnp.concatenate([alive] * (length // 128), axis=1)
    bit = 1
    while bit <= length // 4:
        digit = (start // bit) % 4
        one, two, three = (turned(signal, -bit * times) for times in (1, 2, 3))
        signal = jnp.where(
            digit == 0, signal, jnp.where(digit == 1, one, jnp.where(digit == 2, two, three))
        )
        bit *= 4
    lane = lax.broadcasted_iota(jnp.int32, (rows, length), 1)
    signal = jnp.where(lane + start < length, signal, 0.0)
    power = jnp.concatenate([jnp.abs(signal), jnp.zeros((rows, 2 * widest), jnp.float32)], axis=1)
    half = jnp.concatenate([half] * (power.shape[1] // 128), axis=1)
    total = window_sum(power, half + 1, widest + 1, -1)
    total = total + window_sum(turned(power, 1), half, widest, 1)
    level = total[:, :length] / (2 * half[:, :length] + 1).astype(jnp.float32)
    return signal / (level + tiny)


def whiten_rows(normed, ahead, back, mean):
    length = normed.shape[1]
    half, quarter = length // 2, length // 4
    left, right = normed[:, :half], normed[:, half:]
    even = table_dot(left + right, ahead[0, 0], ahead[1, 0])
    odd = table_dot(left - right, ahead[0, 1], ahead[1, 1])
    even_power = even * even
    odd_power = odd * odd
    magnitude = jnp.sqrt(
        jnp.concatenate(
            [
                even_power[:, :quarter] + even_power[:, quarter:],
                odd_power[:, :quarter] + odd_power[:, quarter:],
            ],
            axis=1,
        )
    )
    smooth = split_dot(three_parts(magnitude), mean) / (2 * smooth_half + 1)
    place = lax.broadcasted_iota(jnp.int32, smooth.shape, 1)
    bins = jnp.where(place < quarter, 2 * place, 2 * (place - quarter) + 1)
    keep = (bins >= length // 250) & (bins <= 2 * length // 5)
    gain = jnp.where(keep, 1.0 / (smooth + tiny), 0.0)
    even_gain, odd_gain = gain[:, :quarter], gain[:, quarter:]
    even = even * jnp.concatenate([even_gain, even_gain], axis=1)
    odd = odd * jnp.concatenate([odd_gain, odd_gain], axis=1)
    even = table_dot(even, back[0, 0], back[1, 0])
    odd = table_dot(odd, back[0, 1], back[1, 1])
    return jnp.concatenate([even + odd, even - odd], axis=1) * (2.0 / math.sqrt(length))


def both_lags(white):
    rows, length = white.shape
    ring = jnp.concatenate([white, jnp.zeros((rows, 2 * LAG), jnp.float32)], axis=1)
    ring = turned(ring, -LAG)
    return jnp.concatenate([ring, turned(ring, 1)], axis=0).astype(jnp.bfloat16)


def fill_lags(both, target, slot, first, last):
    rows = both.shape[0]
    length = target.shape[2]
    for step in range(first, last):
        lagged = turned(both, 2 * step) if step else both
        target[slot, rows * step : rows * (step + 1)] = lagged[:, :length]


def fused_kernel(
    raw, alive_hbm, start_hbm, half_hbm, ahead_hbm, back_hbm, mean_hbm, out,
    alive, seg_start, norm_half, small_sem, own_sem, ahead, back, mean, table_sem, records, params, own, other, lagged, totals,
    raw_send, raw_recv, param_send, param_recv, rail_send, rail_recv, core_send, core_recv,
):
    chan, tm = lax.axis_index("chan"), lax.axis_index("tm")
    depth = lax.axis_size("chan") // 2
    groups = lax.axis_size("tm")
    z, y, x, core = chan // 2, chan % 2, tm // 2, tm % 2
    rows = alive.shape[0]
    pair = 2 * rows
    length = own.shape[2]
    blocks = own.shape[0]

    smalls = [
        pltpu.make_async_copy(source, target, small_sem.at[index])
        for index, (source, target) in enumerate(
            [(alive_hbm, alive), (start_hbm, seg_start), (half_hbm, norm_half)]
        )
    ]
    for load in smalls:
        load.start()
    mine_first = pl.multiple_of(x * pair, pair)
    kept = pltpu.make_async_copy(raw.at[core, pl.ds(mine_first, pair)], records.at[tm], own_sem)
    kept.start()
    loads = [
        pltpu.make_async_copy(source, target, table_sem.at[index])
        for index, (source, target) in enumerate(
            [(ahead_hbm, ahead), (mean_hbm, mean), (back_hbm, back)]
        )
    ]
    for load in loads[:2]:
        load.start()

    near = [z, z + 1 - 2 * (z % 2), z + 2 - 4 * (z // 2), 3 - z]
    others = [(chan, (tm + step) % groups) for step in range(1, groups)]
    along = [(level * 2 + y, tm) for level in near[1:]]
    plane = [
        (y, 1 - x),
        (1 - y, x),
        (1 - y, 1 - x),
    ]
    plane_devices = [(z * 2 + py, px * 2 + core) for py, px in plane]
    barrier = pltpu.get_barrier_semaphore()
    greeted = others + along + plane_devices[1:]
    for device in greeted:
        pl.semaphore_signal(barrier, inc=1, device_id=device, device_id_type=MESH)

    for load in smalls:
        load.wait()
    row_ids = lax.broadcasted_iota(jnp.int32, (rows, 128), 0)
    live = jnp.zeros((rows, 128), jnp.int32)
    half = jnp.zeros((rows, 128), jnp.int32)
    for row in range(rows):
        live = jnp.where(row_ids == row, alive[row], live)
        half = jnp.where(row_ids == row, norm_half[row], half)
    params[core] = jnp.concatenate([live, half], axis=0).astype(jnp.float32)
    pl.semaphore_wait(barrier, len(greeted))

    def remote(source, target, send, receive, device):
        return pltpu.make_async_remote_copy(
            src_ref=source, dst_ref=target, send_sem=send, recv_sem=receive,
            device_id=device, device_id_type=MESH,
        )

    started = []
    for step in range(1, groups):
        peer = (tm + step) % groups
        first = pl.multiple_of((peer // 2) * pair, pair)
        copy = remote(
            raw.at[peer % 2, pl.ds(first, pair)], records.at[tm],
            raw_send.at[step - 1], raw_recv.at[tm], (chan, peer),
        )
        copy.start()
        started.append(copy)
    loads[2].start()
    partner = (chan, x * 2 + 1 - core)
    copy = remote(params.at[core], params.at[core], param_send, param_recv, partner)
    copy.start()
    started.append(copy)
    kept.wait()
    for step in range(1, groups):
        peer = (tm + step) % groups
        remote(
            records.at[peer], records.at[peer], raw_send.at[step - 1], raw_recv.at[peer],
            (chan, peer),
        ).wait_recv()
    remote(
        params.at[1 - core], params.at[1 - core], param_send, param_recv, partner
    ).wait_recv()

    gathered = jnp.concatenate([records[group] for group in range(groups)], axis=1)
    live = jnp.concatenate([params[0, :rows], params[1, :rows]], axis=0)
    half = jnp.concatenate([params[0, rows:], params[1, rows:]], axis=0)
    normed = normed_rows(gathered, seg_start[core], live, half.astype(jnp.int32))
    for load in loads:
        load.wait()
    white = whiten_rows(normed, ahead, back, mean[...]).astype(jnp.bfloat16)

    def block_of(bz, by, bx):
        return (bz * 2 + by) * 2 + bx

    def to_core(block):
        copy = remote(
            own.at[block], other.at[block], core_send.at[block], core_recv.at[block], partner
        )
        copy.start()
        started.append(copy)

    def to_side(block, side, semaphore):
        copy = remote(
            own.at[block], own.at[block], semaphore, rail_recv.at[block], plane_devices[side]
        )
        copy.start()
        started.append(copy)

    def to_plane(block, step):
        for side in range(2):
            to_side(block, side, rail_send.at[step, side])

    def arrived(buffer, semaphores, block):
        remote(
            buffer.at[block], buffer.at[block], core_send.at[block], semaphores.at[block], partner
        ).wait_recv()

    mine = block_of(z, y, x)
    own[mine] = white
    for index, device in enumerate(along):
        copy = remote(
            own.at[mine], own.at[mine], rail_send.at[depth, index], rail_recv.at[mine], device
        )
        copy.start()
        started.append(copy)
    to_plane(mine, 0)
    to_core(mine)

    def from_level(step):
        block = block_of(near[step], y, x)
        arrived(own, rail_recv, block)
        to_plane(block, step)
        to_core(block)

    def from_side(step):
        for side in range(2):
            block = block_of(near[step], *plane[side])
            arrived(own, rail_recv, block)
            if step % 2 == side:
                to_side(block, 1 - side, rail_send.at[step, 2])
            to_core(block)

    def own_rows(block):
        wide = block.astype(jnp.float32)
        return both_lags(jnp.where(core == 0, wide[:rows], wide[rows:]))

    both = own_rows(white)
    fill_lags(both, lagged, 0, 0, LAG // 2)
    from_level(1)
    fill_lags(both, lagged, 0, LAG // 2, LAG + 1)
    from_side(0)
    from_level(2)
    from_side(1)
    from_level(3)
    arrived(other, core_recv, mine)
    fill_lags(own_rows(other[mine]), lagged, 1, 0, LAG + 1)
    from_side(2)
    from_side(3)
    for step in range(depth):
        block = block_of(near[step], *plane[2])
        arrived(own, rail_recv, block)
        to_core(block)

    def lag_dot(slot, columns):
        return lax.dot_general(
            lagged[slot],
            columns[...].reshape(blocks * pair, length),
            (((1,), (1,)), ((), ())),
            preferred_element_type=jnp.float32,
        )

    totals[...] = lag_dot(0, own)
    for step in range(depth):
        for py, px in [(y, x)] + plane:
            if step == 0 and px is x and py is y:
                continue
            arrived(other, core_recv, block_of(near[step], py, px))
    lag_count = out.shape[0]
    shape = (rows, blocks * pair)
    ahead_by = lax.broadcasted_iota(jnp.int32, shape, 1) - (chan * groups + tm) * rows
    same = ahead_by == lax.broadcasted_iota(jnp.int32, shape, 0)
    result = (totals[...] + lag_dot(1, other))[: lag_count * rows].reshape(out.shape)
    result = jnp.where(same[None], 0.0, result * (1.0 / math.sqrt(2 * length)))
    out[...] = result.astype(jnp.bfloat16)
    for copy in started:
        copy.wait_send()


def fused_plan(raw, alive, seg_start, norm_half):
    segs, width, span = raw.shape
    groups, chans = lax.axis_size("tm"), lax.axis_size("chan")
    rows = alive.shape[0]
    length = span * groups
    depth = chans // 2
    blocks = chans * 2
    half = length // 2
    lag_rows = 2 * (LAG + 1) * rows
    ahead, back, mean = transform_tables(length)
    operands = (raw, alive, seg_start, norm_half, ahead, back, mean)
    operands = [jnp.asarray(operand) for operand in operands]
    vmem = pl.BlockSpec(memory_space=pltpu.VMEM)
    hbm = pl.BlockSpec(memory_space=pltpu.HBM)
    dma = pltpu.SemaphoreType.DMA
    corr = pl.pallas_call(
        fused_kernel,
        out_shape=pltpu.VMEM((2 * LAG + 1, rows, width * chans), jnp.bfloat16),
        in_specs=[hbm] * 7,
        out_specs=vmem,
        scratch_shapes=[
            pltpu.SMEM((rows,), jnp.int32),
            pltpu.SMEM((segs,), jnp.int32),
            pltpu.SMEM((rows,), jnp.int32),
            dma((3,)),
            dma(()),
            pltpu.VMEM((2, 2, half, half), jnp.bfloat16),
            pltpu.VMEM((2, 2, half, half), jnp.bfloat16),
            pltpu.VMEM((half, half), jnp.bfloat16),
            dma((3,)),
            pltpu.VMEM((groups, 2 * rows, span), jnp.float32),
            pltpu.VMEM((2, 2 * rows, 128), jnp.float32),
            pltpu.VMEM((blocks, 2 * rows, length), jnp.bfloat16),
            pltpu.VMEM((blocks, 2 * rows, length), jnp.bfloat16),
            pltpu.VMEM((2, lag_rows, length), jnp.bfloat16),
            pltpu.VMEM((lag_rows, width * chans), jnp.float32),
            dma((groups - 1,)),
            dma((groups,)),
            dma(()),
            dma(()),
            dma((depth + 1, 3)),
            dma((blocks,)),
            dma((blocks,)),
            dma((blocks,)),
        ],
        compiler_params=pltpu.CompilerParams(
            collective_id=0, has_side_effects=True, vmem_limit_bytes=48 * 1024 * 1024
        ),
        cost_estimate=pl.CostEstimate(
            flops=4 * lag_rows * length * width * chans,
            bytes_accessed=6 * 1024 * 1024,
            transcendentals=0,
        ),
    )(*[pltpu.with_memory_space_constraint(operand, pltpu.HBM) for operand in operands])
    return jnp.transpose(corr, (1, 0, 2))


def on_device(raw, alive, seg_start, norm_half):
    segs, width, span = raw.shape
    shape = (lax.axis_size("chan"), lax.axis_size("tm"), segs, alive.shape[0], span)
    if shape == (8, 4, 2, 8, 256):
        return fused_plan(raw, alive, seg_start, norm_half)
    return gathered_plan(raw, alive, seg_start, norm_half)


def solution(mesh):
    return jax.shard_map(
        on_device,
        mesh=mesh,
        in_specs=(P(None, "chan", "tm"), P(("chan", "tm")), P(), P(("chan", "tm"))),
        out_specs=P(("chan", "tm"), None, None),
        check_vma=False,
    )
```

```python
import math

import jax
import jax.numpy as jnp
import ml_dtypes
import numpy as np
from jax import lax
from jax.experimental import pallas as pl
from jax.experimental.pallas import tpu as pltpu
from jax.sharding import PartitionSpec as P

LAG = 64


widest = 64
smooth_half = 32
tiny = 1e-05
radix = 128


def window_mean(signal, half_width):
    length = signal.shape[2]
    half = half_width[None, :, None]
    width = 2 * half + 1
    power = jnp.pad(jnp.abs(signal), ((0, 0), (0, 0), (widest, widest)))

    def ahead(value, by):
        return jnp.pad(value[:, :, by:], ((0, 0), (0, 0), (0, by)))

    total = jnp.zeros_like(power)
    span = 1
    while span <= 2 * widest + 1:
        total = jnp.where((width & span) != 0, power + ahead(total, span), total)
        power = power + ahead(power, span)
        span *= 2
    rest = widest - half
    span = 1
    while span <= widest:
        total = jnp.where((rest & span) != 0, ahead(total, span), total)
        span *= 2
    return total[:, :, :length] / width.astype(jnp.float32)


def phase_table(row_total, col_total, modulus):
    product = (
        jnp.arange(row_total, dtype=jnp.int32)[:, None]
        * jnp.arange(col_total, dtype=jnp.int32)[None, :]
        % modulus
    )
    angle = product.astype(jnp.float32) * (2.0 * math.pi / modulus)
    return (jnp.cos(angle), jnp.sin(angle))


def forward_transform(signal, cos_q, sin_q, cos_p, sin_p, cos_t, sin_t):
    length = signal.shape[1]
    inner = length // radix
    highest = lax.Precision.HIGHEST
    grid = signal.reshape(-1, inner, radix)
    first_re = jnp.einsum("rqp,qk->rkp", grid, cos_q, precision=highest)
    first_im = -jnp.einsum("rqp,qk->rkp", grid, sin_q, precision=highest)
    turned_re = first_re * cos_t + first_im * sin_t
    turned_im = first_im * cos_t - first_re * sin_t
    out_re = jnp.einsum("rkp,pj->rjk", turned_re, cos_p, precision=highest) + jnp.einsum(
        "rkp,pj->rjk", turned_im, sin_p, precision=highest
    )
    out_im = jnp.einsum("rkp,pj->rjk", turned_im, cos_p, precision=highest) - jnp.einsum(
        "rkp,pj->rjk", turned_re, sin_p, precision=highest
    )
    return (out_re.reshape(-1, length), out_im.reshape(-1, length))


def inverse_real(spec_re, spec_im, cos_q, sin_q, cos_p, sin_p, cos_t, sin_t):
    length = spec_re.shape[1]
    inner = length // radix
    highest = lax.Precision.HIGHEST
    grid_re = spec_re.reshape(-1, radix, inner)
    grid_im = spec_im.reshape(-1, radix, inner)
    first_re = jnp.einsum("rjk,jp->rkp", grid_re, cos_p, precision=highest) - jnp.einsum(
        "rjk,jp->rkp", grid_im, sin_p, precision=highest
    )
    first_im = jnp.einsum("rjk,jp->rkp", grid_im, cos_p, precision=highest) + jnp.einsum(
        "rjk,jp->rkp", grid_re, sin_p, precision=highest
    )
    turned_re = first_re * cos_t - first_im * sin_t
    turned_im = first_im * cos_t + first_re * sin_t
    result = jnp.einsum("rkp,kq->rqp", turned_re, cos_q, precision=highest) - jnp.einsum(
        "rkp,kq->rqp", turned_im, sin_q, precision=highest
    )
    return result.reshape(-1, length)


def whiten(normed):
    segs, rows, length = normed.shape
    inner = length // radix
    cos_q, sin_q = phase_table(inner, inner, inner)
    cos_p, sin_p = phase_table(radix, radix, radix)
    cos_t, sin_t = phase_table(inner, radix, length)
    spec_re, spec_im = forward_transform(
        normed.reshape(-1, length), cos_q, sin_q, cos_p, sin_p, cos_t, sin_t
    )
    magnitude = jnp.sqrt(spec_re * spec_re + spec_im * spec_im)
    circular = jnp.concatenate(
        [magnitude[:, length - smooth_half :], magnitude, magnitude[:, :smooth_half]], axis=1
    )
    running = jnp.cumsum(circular, axis=1)
    running = jnp.concatenate([jnp.zeros((running.shape[0], 1), jnp.float32), running], axis=1)
    span_bins = 2 * smooth_half + 1
    smooth = (running[:, span_bins:] - running[:, :-span_bins]) / span_bins
    bins = jnp.arange(length, dtype=jnp.int32)
    folded = jnp.minimum(bins, length - bins)
    band = ((folded >= length // 250) & (folded <= 2 * length // 5)).astype(jnp.float32)
    gain = band[None, :] / (smooth + tiny)
    traces = inverse_real(spec_re * gain, spec_im * gain, cos_q, sin_q, cos_p, sin_p, cos_t, sin_t)
    return (traces * (1.0 / math.sqrt(length))).reshape(segs, rows, length).astype(jnp.bfloat16)


def normalised(gathered, alive, seg_start, norm_half):
    segs, rows, length = gathered.shape
    gathered = gathered * alive.astype(jnp.float32)[None, :, None]
    pieces = []
    for segment in range(segs):
        padded = jnp.pad(gathered[segment], ((0, 0), (0, length)))
        pieces.append(lax.dynamic_slice_in_dim(padded, seg_start[segment], length, axis=1))
    signal = jnp.stack(pieces, axis=0)
    return signal / (window_mean(signal, norm_half) + tiny)


def gathered_plan(raw, alive, seg_start, norm_half):
    segs = raw.shape[0]
    rows = alive.shape[0]
    lag_count = 2 * LAG + 1
    device = lax.axis_index("chan") * lax.axis_size("tm") + lax.axis_index("tm")
    pieces = lax.all_to_all(raw, "tm", split_axis=1, concat_axis=2, tiled=True)
    white = whiten(normalised(pieces, alive, seg_start, norm_half))
    length = white.shape[2]
    everyone = lax.all_gather(white, ("chan", "tm"), axis=1, tiled=True)
    padded = jnp.pad(white, ((0, 0), (0, 0), (LAG, LAG)))
    toeplitz = jnp.stack(
        [padded[:, :, 2 * LAG - lag : 2 * LAG - lag + length] for lag in range(lag_count)], axis=2
    )
    total = jnp.einsum("silt,sjt->ilj", toeplitz, everyone, preferred_element_type=jnp.float32)
    row_ids = device * rows + jnp.arange(rows, dtype=jnp.int32)
    col_ids = jnp.arange(everyone.shape[1], dtype=jnp.int32)
    keep = row_ids[:, None, None] != col_ids[None, None, :]
    scaled = total * (1.0 / math.sqrt(segs * length))
    return jnp.where(keep, scaled, 0.0).astype(jnp.bfloat16)


MESH = pl.DeviceIdType.MESH


def two_parts(table):
    high = table.astype(ml_dtypes.bfloat16)
    low = (table - high.astype(np.float64)).astype(ml_dtypes.bfloat16)
    return np.stack([high, low])


def transform_tables(length):
    half, quarter = length // 2, length // 4
    moments = np.arange(half)
    low_bin, high_bin = length // 250, 2 * length // 5
    ahead, back = [], []
    for parity in range(2):
        bins = 2 * np.arange(quarter) + parity
        angle = 2.0 * np.pi * ((moments[:, None] * bins[None, :]) % length) / length
        ahead.append(np.concatenate([np.cos(angle), -np.sin(angle)], axis=1))
        back.append(np.concatenate([np.cos(angle), -np.sin(angle)], axis=1).T)
    order = np.concatenate([np.arange(0, half, 2), np.arange(1, half, 2)])
    place = np.empty(half, np.int64)
    place[order] = np.arange(half)
    mean = np.zeros((half, half), np.float32)
    for column, bin_index in enumerate(order):
        if low_bin <= bin_index <= high_bin:
            for offset in range(-smooth_half, smooth_half + 1):
                mean[place[abs(bin_index + offset)], column] += 1.0
    return (
        two_parts(np.stack(ahead)),
        two_parts(np.stack(back)),
        mean.astype(ml_dtypes.bfloat16),
    )


def three_parts(value):
    high = value.astype(jnp.bfloat16)
    rest = value - high.astype(jnp.float32)
    middle = rest.astype(jnp.bfloat16)
    low = (rest - middle.astype(jnp.float32)).astype(jnp.bfloat16)
    return jnp.concatenate([high, middle, low], axis=0)


def split_dot(parts, table):
    rows = parts.shape[0] // 3
    result = jnp.dot(parts, table, preferred_element_type=jnp.float32)
    return result[2 * rows :] + result[rows : 2 * rows] + result[:rows]


def table_dot(value, high, low):
    parts = three_parts(value)
    return split_dot(parts, low) + split_dot(parts, high)


def turned(value, by):
    length = value.shape[1]
    return pltpu.roll(value, by % length, 1)


def window_sum(first, count, limit, way):
    power = first
    total = jnp.where((count & 1) != 0, power, 0.0)
    bit = 1
    while 2 * bit <= limit:
        power = power + turned(power, way * bit)
        bit *= 2
        total = jnp.where((count & bit) != 0, power + turned(total, way * bit), total)
    return total


def normed_rows(records, start, alive, half):
    rows, length = records.shape
    signal = records * jnp.concatenate([alive] * (length // 128), axis=1)
    bit = 1
    while bit <= length // 4:
        digit = (start // bit) % 4
        one, two, three = (turned(signal, -bit * times) for times in (1, 2, 3))
        signal = jnp.where(
            digit == 0, signal, jnp.where(digit == 1, one, jnp.where(digit == 2, two, three))
        )
        bit *= 4
    lane = lax.broadcasted_iota(jnp.int32, (rows, length), 1)
    signal = jnp.where(lane + start < length, signal, 0.0)
    power = jnp.concatenate([jnp.abs(signal), jnp.zeros((rows, 2 * widest), jnp.float32)], axis=1)
    half = jnp.concatenate([half] * (power.shape[1] // 128), axis=1)
    total = window_sum(power, half + 1, widest + 1, -1)
    total = total + window_sum(turned(power, 1), half, widest, 1)
    level = total[:, :length] / (2 * half[:, :length] + 1).astype(jnp.float32)
    return signal / (level + tiny)


def whiten_rows(normed, ahead, back, mean, ready):
    length = normed.shape[1]
    half, quarter = length // 2, length // 4
    left, right = normed[:, :half], normed[:, half:]
    even = table_dot(left + right, ahead[0, 0], ahead[1, 0])
    odd = table_dot(left - right, ahead[0, 1], ahead[1, 1])
    even_power = even * even
    odd_power = odd * odd
    magnitude = jnp.sqrt(
        jnp.concatenate(
            [
                even_power[:, :quarter] + even_power[:, quarter:],
                odd_power[:, :quarter] + odd_power[:, quarter:],
            ],
            axis=1,
        )
    )
    smooth = split_dot(three_parts(magnitude), mean) / (2 * smooth_half + 1)
    place = lax.broadcasted_iota(jnp.int32, smooth.shape, 1)
    bins = jnp.where(place < quarter, 2 * place, 2 * (place - quarter) + 1)
    keep = (bins >= length // 250) & (bins <= 2 * length // 5)
    gain = jnp.where(keep, 1.0 / (smooth + tiny), 0.0)
    even_gain, odd_gain = gain[:, :quarter], gain[:, quarter:]
    even = even * jnp.concatenate([even_gain, even_gain], axis=1)
    odd = odd * jnp.concatenate([odd_gain, odd_gain], axis=1)
    ready()
    even = table_dot(even, back[0, 0], back[1, 0])
    odd = table_dot(odd, back[0, 1], back[1, 1])
    return jnp.concatenate([even + odd, even - odd], axis=1) * (2.0 / math.sqrt(length))


def both_lags(white):
    rows, length = white.shape
    ring = jnp.concatenate([white, jnp.zeros((rows, 2 * LAG), jnp.float32)], axis=1)
    ring = turned(ring, -LAG)
    return jnp.concatenate([ring, turned(ring, 1)], axis=0).astype(jnp.bfloat16)


def fill_lags(both, target, slot, first, last):
    rows = both.shape[0]
    length = target.shape[2]
    for step in range(first, last):
        lagged = turned(both, 2 * step) if step else both
        target[slot, rows * step : rows * (step + 1)] = lagged[:, :length]


def fused_kernel(
    raw, alive_hbm, start_hbm, half_hbm, ahead_hbm, back_hbm, mean_hbm, out,
    alive, seg_start, norm_half, small_sem, own_sem, ahead, back, mean, table_sem, records, params, own, other, lagged, totals,
    raw_send, raw_recv, param_send, param_recv, rail_send, rail_recv, core_send, core_recv,
):
    chan, tm = lax.axis_index("chan"), lax.axis_index("tm")
    depth = lax.axis_size("chan") // 2
    groups = lax.axis_size("tm")
    z, y, x, core = chan // 2, chan % 2, tm // 2, tm % 2
    rows = alive.shape[0]
    pair = 2 * rows
    length = own.shape[2]
    blocks = own.shape[0]

    smalls = [
        pltpu.make_async_copy(source, target, small_sem.at[index])
        for index, (source, target) in enumerate(
            [(alive_hbm, alive), (start_hbm, seg_start), (half_hbm, norm_half)]
        )
    ]
    for load in smalls:
        load.start()
    mine_first = pl.multiple_of(x * pair, pair)
    kept = pltpu.make_async_copy(raw.at[core, pl.ds(mine_first, pair)], records.at[tm], own_sem)
    kept.start()
    loads = [
        pltpu.make_async_copy(source, target, table_sem.at[index])
        for index, (source, target) in enumerate(
            [(ahead_hbm, ahead), (mean_hbm, mean), (back_hbm, back)]
        )
    ]
    for load in loads[:2]:
        load.start()

    near = [z, z + 1 - 2 * (z % 2), z + 2 - 4 * (z // 2), 3 - z]
    others = [(chan, (tm + step) % groups) for step in range(1, groups)]
    along = [(level * 2 + y, tm) for level in near[1:]]
    plane = [
        (y, 1 - x),
        (1 - y, x),
        (1 - y, 1 - x),
    ]
    plane_devices = [(z * 2 + py, px * 2 + core) for py, px in plane]
    barrier = pltpu.get_barrier_semaphore()
    greeted = others + along + plane_devices[1:]
    for device in greeted:
        pl.semaphore_signal(barrier, inc=1, device_id=device, device_id_type=MESH)

    for load in smalls:
        load.wait()
    row_ids = lax.broadcasted_iota(jnp.int32, (rows, 128), 0)
    live = jnp.zeros((rows, 128), jnp.int32)
    half = jnp.zeros((rows, 128), jnp.int32)
    for row in range(rows):
        live = jnp.where(row_ids == row, alive[row], live)
        half = jnp.where(row_ids == row, norm_half[row], half)
    params[core] = jnp.concatenate([live, half], axis=0).astype(jnp.float32)
    pl.semaphore_wait(barrier, len(greeted))

    def remote(source, target, send, receive, device):
        return pltpu.make_async_remote_copy(
            src_ref=source, dst_ref=target, send_sem=send, recv_sem=receive,
            device_id=device, device_id_type=MESH,
        )

    started = []
    for step in range(1, groups):
        peer = (tm + step) % groups
        first = pl.multiple_of((peer // 2) * pair, pair)
        copy = remote(
            raw.at[peer % 2, pl.ds(first, pair)], records.at[tm],
            raw_send.at[step - 1], raw_recv.at[tm], (chan, peer),
        )
        copy.start()
        started.append(copy)
    loads[2].start()
    partner = (chan, x * 2 + 1 - core)
    copy = remote(params.at[core], params.at[core], param_send, param_recv, partner)
    copy.start()
    started.append(copy)
    kept.wait()
    for step in range(1, groups):
        peer = (tm + step) % groups
        remote(
            records.at[peer], records.at[peer], raw_send.at[step - 1], raw_recv.at[peer],
            (chan, peer),
        ).wait_recv()
    remote(
        params.at[1 - core], params.at[1 - core], param_send, param_recv, partner
    ).wait_recv()

    gathered = jnp.concatenate([records[group] for group in range(groups)], axis=1)
    live = jnp.concatenate([params[0, :rows], params[1, :rows]], axis=0)
    half = jnp.concatenate([params[0, rows:], params[1, rows:]], axis=0)
    normed = normed_rows(gathered, seg_start[core], live, half.astype(jnp.int32))
    for load in loads[:2]:
        load.wait()
    white = whiten_rows(normed, ahead, back, mean[...], loads[2].wait).astype(jnp.bfloat16)

    def block_of(bz, by, bx):
        return (bz * 2 + by) * 2 + bx

    def to_core(block):
        copy = remote(
            own.at[block], other.at[block], core_send.at[block], core_recv.at[block], partner
        )
        copy.start()
        started.append(copy)

    def to_side(block, side, semaphore):
        copy = remote(
            own.at[block], own.at[block], semaphore, rail_recv.at[block], plane_devices[side]
        )
        copy.start()
        started.append(copy)

    def to_plane(block, step):
        for side in range(2):
            to_side(block, side, rail_send.at[step, side])

    def arrived(buffer, semaphores, block):
        remote(
            buffer.at[block], buffer.at[block], core_send.at[block], semaphores.at[block], partner
        ).wait_recv()

    mine = block_of(z, y, x)
    own[mine] = white
    for index, device in enumerate(along):
        copy = remote(
            own.at[mine], own.at[mine], rail_send.at[depth, index], rail_recv.at[mine], device
        )
        copy.start()
        started.append(copy)
    to_plane(mine, 0)
    to_core(mine)

    def from_level(step):
        block = block_of(near[step], y, x)
        arrived(own, rail_recv, block)
        to_plane(block, step)
        to_core(block)

    def from_side(step):
        for side in range(2):
            block = block_of(near[step], *plane[side])
            arrived(own, rail_recv, block)
            if step % 2 == side:
                to_side(block, 1 - side, rail_send.at[step, 2])
            to_core(block)

    def own_rows(block):
        wide = block.astype(jnp.float32)
        return both_lags(jnp.where(core == 0, wide[:rows], wide[rows:]))

    both = own_rows(white)
    fill_lags(both, lagged, 0, 0, LAG + 1)
    for step in range(1, depth):
        from_level(step)
    arrived(other, core_recv, mine)
    fill_lags(own_rows(other[mine]), lagged, 1, 0, LAG + 1)
    for step in range(depth):
        from_side(step)
    for step in range(depth):
        block = block_of(near[step], *plane[2])
        arrived(own, rail_recv, block)
        to_core(block)

    def lag_dot(slot, columns):
        return lax.dot_general(
            lagged[slot],
            columns[...].reshape(blocks * pair, length),
            (((1,), (1,)), ((), ())),
            preferred_element_type=jnp.float32,
        )

    totals[...] = lag_dot(0, own)
    for step in range(depth):
        for py, px in [(y, x)] + plane:
            if step == 0 and px is x and py is y:
                continue
            arrived(other, core_recv, block_of(near[step], py, px))
    lag_count = out.shape[0]
    shape = (rows, blocks * pair)
    ahead_by = lax.broadcasted_iota(jnp.int32, shape, 1) - (chan * groups + tm) * rows
    same = ahead_by == lax.broadcasted_iota(jnp.int32, shape, 0)
    result = (totals[...] + lag_dot(1, other))[: lag_count * rows].reshape(out.shape)
    result = jnp.where(same[None], 0.0, result * (1.0 / math.sqrt(2 * length)))
    out[...] = result.astype(jnp.bfloat16)
    for copy in started:
        copy.wait_send()


def fused_plan(raw, alive, seg_start, norm_half):
    segs, width, span = raw.shape
    groups, chans = lax.axis_size("tm"), lax.axis_size("chan")
    rows = alive.shape[0]
    length = span * groups
    depth = chans // 2
    blocks = chans * 2
    half = length // 2
    lag_rows = 2 * (LAG + 1) * rows
    ahead, back, mean = transform_tables(length)
    operands = (raw, alive, seg_start, norm_half, ahead, back, mean)
    operands = [jnp.asarray(operand) for operand in operands]
    vmem = pl.BlockSpec(memory_space=pltpu.VMEM)
    hbm = pl.BlockSpec(memory_space=pltpu.HBM)
    dma = pltpu.SemaphoreType.DMA
    corr = pl.pallas_call(
        fused_kernel,
        out_shape=pltpu.VMEM((2 * LAG + 1, rows, width * chans), jnp.bfloat16),
        in_specs=[hbm] * 7,
        out_specs=vmem,
        scratch_shapes=[
            pltpu.SMEM((rows,), jnp.int32),
            pltpu.SMEM((segs,), jnp.int32),
            pltpu.SMEM((rows,), jnp.int32),
            dma((3,)),
            dma(()),
            pltpu.VMEM((2, 2, half, half), jnp.bfloat16),
            pltpu.VMEM((2, 2, half, half), jnp.bfloat16),
            pltpu.VMEM((half, half), jnp.bfloat16),
            dma((3,)),
            pltpu.VMEM((groups, 2 * rows, span), jnp.float32),
            pltpu.VMEM((2, 2 * rows, 128), jnp.float32),
            pltpu.VMEM((blocks, 2 * rows, length), jnp.bfloat16),
            pltpu.VMEM((blocks, 2 * rows, length), jnp.bfloat16),
            pltpu.VMEM((2, lag_rows, length), jnp.bfloat16),
            pltpu.VMEM((lag_rows, width * chans), jnp.float32),
            dma((groups - 1,)),
            dma((groups,)),
            dma(()),
            dma(()),
            dma((depth + 1, 3)),
            dma((blocks,)),
            dma((blocks,)),
            dma((blocks,)),
        ],
        compiler_params=pltpu.CompilerParams(
            collective_id=0, has_side_effects=True, vmem_limit_bytes=48 * 1024 * 1024
        ),
        cost_estimate=pl.CostEstimate(
            flops=4 * lag_rows * length * width * chans,
            bytes_accessed=6 * 1024 * 1024,
            transcendentals=0,
        ),
    )(*[pltpu.with_memory_space_constraint(operand, pltpu.HBM) for operand in operands])
    return jnp.transpose(corr, (1, 0, 2))


def on_device(raw, alive, seg_start, norm_half):
    segs, width, span = raw.shape
    shape = (lax.axis_size("chan"), lax.axis_size("tm"), segs, alive.shape[0], span)
    if shape == (8, 4, 2, 8, 256):
        return fused_plan(raw, alive, seg_start, norm_half)
    return gathered_plan(raw, alive, seg_start, norm_half)


def solution(mesh):
    return jax.shard_map(
        on_device,
        mesh=mesh,
        in_specs=(P(None, "chan", "tm"), P(("chan", "tm")), P(), P(("chan", "tm"))),
        out_specs=P(("chan", "tm"), None, None),
        check_vma=False,
    )
```

```python
import math

import jax
import jax.numpy as jnp
import ml_dtypes
import numpy as np
from jax import lax
from jax.experimental import pallas as pl
from jax.experimental.pallas import tpu as pltpu
from jax.sharding import PartitionSpec as P

LAG = 64


widest = 64
smooth_half = 32
tiny = 1e-05
radix = 128


def window_mean(signal, half_width):
    length = signal.shape[2]
    half = half_width[None, :, None]
    width = 2 * half + 1
    power = jnp.pad(jnp.abs(signal), ((0, 0), (0, 0), (widest, widest)))

    def ahead(value, by):
        return jnp.pad(value[:, :, by:], ((0, 0), (0, 0), (0, by)))

    total = jnp.zeros_like(power)
    span = 1
    while span <= 2 * widest + 1:
        total = jnp.where((width & span) != 0, power + ahead(total, span), total)
        power = power + ahead(power, span)
        span *= 2
    rest = widest - half
    span = 1
    while span <= widest:
        total = jnp.where((rest & span) != 0, ahead(total, span), total)
        span *= 2
    return total[:, :, :length] / width.astype(jnp.float32)


def phase_table(row_total, col_total, modulus):
    product = (
        jnp.arange(row_total, dtype=jnp.int32)[:, None]
        * jnp.arange(col_total, dtype=jnp.int32)[None, :]
        % modulus
    )
    angle = product.astype(jnp.float32) * (2.0 * math.pi / modulus)
    return (jnp.cos(angle), jnp.sin(angle))


def forward_transform(signal, cos_q, sin_q, cos_p, sin_p, cos_t, sin_t):
    length = signal.shape[1]
    inner = length // radix
    highest = lax.Precision.HIGHEST
    grid = signal.reshape(-1, inner, radix)
    first_re = jnp.einsum("rqp,qk->rkp", grid, cos_q, precision=highest)
    first_im = -jnp.einsum("rqp,qk->rkp", grid, sin_q, precision=highest)
    turned_re = first_re * cos_t + first_im * sin_t
    turned_im = first_im * cos_t - first_re * sin_t
    out_re = jnp.einsum("rkp,pj->rjk", turned_re, cos_p, precision=highest) + jnp.einsum(
        "rkp,pj->rjk", turned_im, sin_p, precision=highest
    )
    out_im = jnp.einsum("rkp,pj->rjk", turned_im, cos_p, precision=highest) - jnp.einsum(
        "rkp,pj->rjk", turned_re, sin_p, precision=highest
    )
    return (out_re.reshape(-1, length), out_im.reshape(-1, length))


def inverse_real(spec_re, spec_im, cos_q, sin_q, cos_p, sin_p, cos_t, sin_t):
    length = spec_re.shape[1]
    inner = length // radix
    highest = lax.Precision.HIGHEST
    grid_re = spec_re.reshape(-1, radix, inner)
    grid_im = spec_im.reshape(-1, radix, inner)
    first_re = jnp.einsum("rjk,jp->rkp", grid_re, cos_p, precision=highest) - jnp.einsum(
        "rjk,jp->rkp", grid_im, sin_p, precision=highest
    )
    first_im = jnp.einsum("rjk,jp->rkp", grid_im, cos_p, precision=highest) + jnp.einsum(
        "rjk,jp->rkp", grid_re, sin_p, precision=highest
    )
    turned_re = first_re * cos_t - first_im * sin_t
    turned_im = first_im * cos_t + first_re * sin_t
    result = jnp.einsum("rkp,kq->rqp", turned_re, cos_q, precision=highest) - jnp.einsum(
        "rkp,kq->rqp", turned_im, sin_q, precision=highest
    )
    return result.reshape(-1, length)


def whiten(normed):
    segs, rows, length = normed.shape
    inner = length // radix
    cos_q, sin_q = phase_table(inner, inner, inner)
    cos_p, sin_p = phase_table(radix, radix, radix)
    cos_t, sin_t = phase_table(inner, radix, length)
    spec_re, spec_im = forward_transform(
        normed.reshape(-1, length), cos_q, sin_q, cos_p, sin_p, cos_t, sin_t
    )
    magnitude = jnp.sqrt(spec_re * spec_re + spec_im * spec_im)
    circular = jnp.concatenate(
        [magnitude[:, length - smooth_half :], magnitude, magnitude[:, :smooth_half]], axis=1
    )
    running = jnp.cumsum(circular, axis=1)
    running = jnp.concatenate([jnp.zeros((running.shape[0], 1), jnp.float32), running], axis=1)
    span_bins = 2 * smooth_half + 1
    smooth = (running[:, span_bins:] - running[:, :-span_bins]) / span_bins
    bins = jnp.arange(length, dtype=jnp.int32)
    folded = jnp.minimum(bins, length - bins)
    band = ((folded >= length // 250) & (folded <= 2 * length // 5)).astype(jnp.float32)
    gain = band[None, :] / (smooth + tiny)
    traces = inverse_real(spec_re * gain, spec_im * gain, cos_q, sin_q, cos_p, sin_p, cos_t, sin_t)
    return (traces * (1.0 / math.sqrt(length))).reshape(segs, rows, length).astype(jnp.bfloat16)


def normalised(gathered, alive, seg_start, norm_half):
    segs, rows, length = gathered.shape
    gathered = gathered * alive.astype(jnp.float32)[None, :, None]
    pieces = []
    for segment in range(segs):
        padded = jnp.pad(gathered[segment], ((0, 0), (0, length)))
        pieces.append(lax.dynamic_slice_in_dim(padded, seg_start[segment], length, axis=1))
    signal = jnp.stack(pieces, axis=0)
    return signal / (window_mean(signal, norm_half) + tiny)


def gathered_plan(raw, alive, seg_start, norm_half):
    segs = raw.shape[0]
    rows = alive.shape[0]
    lag_count = 2 * LAG + 1
    device = lax.axis_index("chan") * lax.axis_size("tm") + lax.axis_index("tm")
    pieces = lax.all_to_all(raw, "tm", split_axis=1, concat_axis=2, tiled=True)
    white = whiten(normalised(pieces, alive, seg_start, norm_half))
    length = white.shape[2]
    everyone = lax.all_gather(white, ("chan", "tm"), axis=1, tiled=True)
    padded = jnp.pad(white, ((0, 0), (0, 0), (LAG, LAG)))
    toeplitz = jnp.stack(
        [padded[:, :, 2 * LAG - lag : 2 * LAG - lag + length] for lag in range(lag_count)], axis=2
    )
    total = jnp.einsum("silt,sjt->ilj", toeplitz, everyone, preferred_element_type=jnp.float32)
    row_ids = device * rows + jnp.arange(rows, dtype=jnp.int32)
    col_ids = jnp.arange(everyone.shape[1], dtype=jnp.int32)
    keep = row_ids[:, None, None] != col_ids[None, None, :]
    scaled = total * (1.0 / math.sqrt(segs * length))
    return jnp.where(keep, scaled, 0.0).astype(jnp.bfloat16)


MESH = pl.DeviceIdType.MESH


def two_parts(table):
    high = table.astype(ml_dtypes.bfloat16)
    low = (table - high.astype(np.float64)).astype(ml_dtypes.bfloat16)
    return np.stack([high, low])


def transform_tables(length):
    half, quarter = length // 2, length // 4
    moments = np.arange(half)
    low_bin, high_bin = length // 250, 2 * length // 5
    ahead, back = [], []
    for parity in range(2):
        bins = 2 * np.arange(quarter) + parity
        angle = 2.0 * np.pi * ((moments[:, None] * bins[None, :]) % length) / length
        ahead.append(np.concatenate([np.cos(angle), -np.sin(angle)], axis=1))
        back.append(np.concatenate([np.cos(angle), -np.sin(angle)], axis=1).T)
    order = np.concatenate([np.arange(0, half, 2), np.arange(1, half, 2)])
    place = np.empty(half, np.int64)
    place[order] = np.arange(half)
    mean = np.zeros((half, half), np.float32)
    for column, bin_index in enumerate(order):
        if low_bin <= bin_index <= high_bin:
            for offset in range(-smooth_half, smooth_half + 1):
                mean[place[abs(bin_index + offset)], column] += 1.0
    return (
        two_parts(np.stack(ahead)),
        two_parts(np.stack(back)),
        mean.astype(ml_dtypes.bfloat16),
    )


def three_parts(value):
    high = value.astype(jnp.bfloat16)
    rest = value - high.astype(jnp.float32)
    middle = rest.astype(jnp.bfloat16)
    low = (rest - middle.astype(jnp.float32)).astype(jnp.bfloat16)
    return jnp.concatenate([high, middle, low], axis=0)


def split_dot(parts, table):
    rows = parts.shape[0] // 3
    result = jnp.dot(parts, table, preferred_element_type=jnp.float32)
    return result[2 * rows :] + result[rows : 2 * rows] + result[:rows]


def table_dot(value, high, low):
    parts = three_parts(value)
    return split_dot(parts, low) + split_dot(parts, high)


def turned(value, by):
    length = value.shape[1]
    return pltpu.roll(value, by % length, 1)


def window_sum(first, count, limit, way):
    power = first
    total = jnp.where((count & 1) != 0, power, 0.0)
    bit = 1
    while 2 * bit <= limit:
        power = power + turned(power, way * bit)
        bit *= 2
        total = jnp.where((count & bit) != 0, power + turned(total, way * bit), total)
    return total


def normed_rows(records, start, alive, half):
    rows, length = records.shape
    signal = records * jnp.concatenate([alive] * (length // 128), axis=1)
    bit = 1
    while bit <= length // 4:
        digit = (start // bit) % 4
        one, two, three = (turned(signal, -bit * times) for times in (1, 2, 3))
        signal = jnp.where(
            digit == 0, signal, jnp.where(digit == 1, one, jnp.where(digit == 2, two, three))
        )
        bit *= 4
    lane = lax.broadcasted_iota(jnp.int32, (rows, length), 1)
    signal = jnp.where(lane + start < length, signal, 0.0)
    power = jnp.concatenate([jnp.abs(signal), jnp.zeros((rows, 2 * widest), jnp.float32)], axis=1)
    half = jnp.concatenate([half] * (power.shape[1] // 128), axis=1)
    total = window_sum(power, half + 1, widest + 1, -1)
    total = total + window_sum(turned(power, 1), half, widest, 1)
    level = total[:, :length] / (2 * half[:, :length] + 1).astype(jnp.float32)
    return signal / (level + tiny)


def whiten_rows(normed, ahead, back, mean, ready):
    length = normed.shape[1]
    half, quarter = length // 2, length // 4
    left, right = normed[:, :half], normed[:, half:]
    even = table_dot(left + right, ahead[0, 0], ahead[1, 0])
    odd = table_dot(left - right, ahead[0, 1], ahead[1, 1])
    even_power = even * even
    odd_power = odd * odd
    magnitude = jnp.sqrt(
        jnp.concatenate(
            [
                even_power[:, :quarter] + even_power[:, quarter:],
                odd_power[:, :quarter] + odd_power[:, quarter:],
            ],
            axis=1,
        )
    )
    smooth = split_dot(three_parts(magnitude), mean) / (2 * smooth_half + 1)
    place = lax.broadcasted_iota(jnp.int32, smooth.shape, 1)
    bins = jnp.where(place < quarter, 2 * place, 2 * (place - quarter) + 1)
    keep = (bins >= length // 250) & (bins <= 2 * length // 5)
    gain = jnp.where(keep, 1.0 / (smooth + tiny), 0.0)
    even_gain, odd_gain = gain[:, :quarter], gain[:, quarter:]
    even = even * jnp.concatenate([even_gain, even_gain], axis=1)
    odd = odd * jnp.concatenate([odd_gain, odd_gain], axis=1)
    ready()
    even = table_dot(even, back[0, 0], back[1, 0])
    odd = table_dot(odd, back[0, 1], back[1, 1])
    return jnp.concatenate([even + odd, even - odd], axis=1) * (2.0 / math.sqrt(length))


def both_lags(white):
    rows, length = white.shape
    ring = jnp.concatenate([white, jnp.zeros((rows, 2 * LAG), jnp.float32)], axis=1)
    ring = turned(ring, -LAG)
    return jnp.concatenate([ring, turned(ring, 1)], axis=0).astype(jnp.bfloat16)


def fill_lags(both, target, slot, first, last):
    rows = both.shape[0]
    length = target.shape[2]
    for step in range(first, last):
        lagged = turned(both, 2 * step) if step else both
        target[slot, rows * step : rows * (step + 1)] = lagged[:, :length]


def fused_kernel(
    raw, alive_hbm, start_hbm, half_hbm, ahead_hbm, back_hbm, mean_hbm, out,
    alive, seg_start, norm_half, small_sem, own_sem, ahead, back, mean, table_sem, records, params, own, other, lagged, totals,
    raw_send, raw_recv, param_send, param_recv, rail_send, rail_recv, core_send, core_recv,
):
    chan, tm = lax.axis_index("chan"), lax.axis_index("tm")
    depth = lax.axis_size("chan") // 2
    groups = lax.axis_size("tm")
    z, y, x, core = chan // 2, chan % 2, tm // 2, tm % 2
    rows = alive.shape[0]
    pair = 2 * rows
    length = own.shape[2]
    blocks = own.shape[0]

    smalls = [
        pltpu.make_async_copy(source, target, small_sem.at[index])
        for index, (source, target) in enumerate(
            [(alive_hbm, alive), (start_hbm, seg_start), (half_hbm, norm_half)]
        )
    ]
    for load in smalls:
        load.start()
    mine_first = pl.multiple_of(x * pair, pair)
    kept = pltpu.make_async_copy(raw.at[core, pl.ds(mine_first, pair)], records.at[tm], own_sem)
    kept.start()
    loads = [
        pltpu.make_async_copy(source, target, table_sem.at[index])
        for index, (source, target) in enumerate(
            [(ahead_hbm, ahead), (mean_hbm, mean), (back_hbm, back)]
        )
    ]
    for load in loads[:2]:
        load.start()

    near = [z, z + 1 - 2 * (z % 2), z + 2 - 4 * (z // 2), 3 - z]
    others = [(chan, (tm + step) % groups) for step in range(1, groups)]
    along = [(level * 2 + y, tm) for level in near[1:]]
    plane = [
        (y, 1 - x),
        (1 - y, x),
        (1 - y, 1 - x),
    ]
    plane_devices = [(z * 2 + py, px * 2 + core) for py, px in plane]
    barrier = pltpu.get_barrier_semaphore()
    greeted = others + along + plane_devices[1:]
    for device in greeted:
        pl.semaphore_signal(barrier, inc=1, device_id=device, device_id_type=MESH)

    for load in smalls:
        load.wait()
    row_ids = lax.broadcasted_iota(jnp.int32, (rows, 128), 0)
    live = jnp.zeros((rows, 128), jnp.int32)
    half = jnp.zeros((rows, 128), jnp.int32)
    for row in range(rows):
        live = jnp.where(row_ids == row, alive[row], live)
        half = jnp.where(row_ids == row, norm_half[row], half)
    params[core] = jnp.concatenate([live, half], axis=0).astype(jnp.float32)
    pl.semaphore_wait(barrier, len(greeted))

    def remote(source, target, send, receive, device):
        return pltpu.make_async_remote_copy(
            src_ref=source, dst_ref=target, send_sem=send, recv_sem=receive,
            device_id=device, device_id_type=MESH,
        )

    started = []
    for step in range(1, groups):
        peer = (tm + step) % groups
        first = pl.multiple_of((peer // 2) * pair, pair)
        copy = remote(
            raw.at[peer % 2, pl.ds(first, pair)], records.at[tm],
            raw_send.at[step - 1], raw_recv.at[tm], (chan, peer),
        )
        copy.start()
        started.append(copy)
    loads[2].start()
    partner = (chan, x * 2 + 1 - core)
    copy = remote(params.at[core], params.at[core], param_send, param_recv, partner)
    copy.start()
    started.append(copy)
    kept.wait()
    for step in range(1, groups):
        peer = (tm + step) % groups
        remote(
            records.at[peer], records.at[peer], raw_send.at[step - 1], raw_recv.at[peer],
            (chan, peer),
        ).wait_recv()
    remote(
        params.at[1 - core], params.at[1 - core], param_send, param_recv, partner
    ).wait_recv()

    gathered = jnp.concatenate([records[group] for group in range(groups)], axis=1)
    live = jnp.concatenate([params[0, :rows], params[1, :rows]], axis=0)
    half = jnp.concatenate([params[0, rows:], params[1, rows:]], axis=0)
    normed = normed_rows(gathered, seg_start[core], live, half.astype(jnp.int32))
    for load in loads[:2]:
        load.wait()
    white = whiten_rows(normed, ahead, back, mean[...], loads[2].wait).astype(jnp.bfloat16)

    def block_of(bz, by, bx):
        return (bz * 2 + by) * 2 + bx

    def to_core(block):
        copy = remote(
            own.at[block], other.at[block], core_send.at[block], core_recv.at[block], partner
        )
        copy.start()
        started.append(copy)

    def to_side(block, side, semaphore):
        copy = remote(
            own.at[block], own.at[block], semaphore, rail_recv.at[block], plane_devices[side]
        )
        copy.start()
        started.append(copy)

    def to_plane(block, step):
        for side in range(2):
            to_side(block, side, rail_send.at[step, side])

    def arrived(buffer, semaphores, block):
        remote(
            buffer.at[block], buffer.at[block], core_send.at[block], semaphores.at[block], partner
        ).wait_recv()

    mine = block_of(z, y, x)
    own[mine] = white
    for index, device in enumerate(along):
        copy = remote(
            own.at[mine], own.at[mine], rail_send.at[depth, index], rail_recv.at[mine], device
        )
        copy.start()
        started.append(copy)
    to_plane(mine, 0)
    to_core(mine)

    def from_level(step):
        block = block_of(near[step], y, x)
        arrived(own, rail_recv, block)
        to_plane(block, step)
        to_core(block)

    def from_side(step):
        for side in range(2):
            block = block_of(near[step], *plane[side])
            arrived(own, rail_recv, block)
            if step % 2 == side:
                to_side(block, 1 - side, rail_send.at[step, 2])
            to_core(block)

    def own_rows(block):
        wide = block.astype(jnp.float32)
        return both_lags(jnp.where(core == 0, wide[:rows], wide[rows:]))

    both = own_rows(white)
    fill_lags(both, lagged, 0, 0, LAG // 2)
    from_level(1)
    fill_lags(both, lagged, 0, LAG // 2, LAG + 1)
    for step in range(2, depth):
        from_level(step)
    for step in range(2):
        from_side(step)
    arrived(other, core_recv, mine)
    fill_lags(own_rows(other[mine]), lagged, 1, 0, LAG + 1)
    for step in range(2, depth):
        from_side(step)
    for step in range(depth):
        block = block_of(near[step], *plane[2])
        arrived(own, rail_recv, block)
        to_core(block)

    def lag_dot(slot, columns):
        return lax.dot_general(
            lagged[slot],
            columns[...].reshape(blocks * pair, length),
            (((1,), (1,)), ((), ())),
            preferred_element_type=jnp.float32,
        )

    totals[...] = lag_dot(0, own)
    for step in range(depth):
        for py, px in [(y, x)] + plane:
            if step == 0 and px is x and py is y:
                continue
            arrived(other, core_recv, block_of(near[step], py, px))
    lag_count = out.shape[0]
    shape = (rows, blocks * pair)
    ahead_by = lax.broadcasted_iota(jnp.int32, shape, 1) - (chan * groups + tm) * rows
    same = ahead_by == lax.broadcasted_iota(jnp.int32, shape, 0)
    result = (totals[...] + lag_dot(1, other))[: lag_count * rows].reshape(out.shape)
    result = jnp.where(same[None], 0.0, result * (1.0 / math.sqrt(2 * length)))
    out[...] = result.astype(jnp.bfloat16)
    for copy in started:
        copy.wait_send()


def fused_plan(raw, alive, seg_start, norm_half):
    segs, width, span = raw.shape
    groups, chans = lax.axis_size("tm"), lax.axis_size("chan")
    rows = alive.shape[0]
    length = span * groups
    depth = chans // 2
    blocks = chans * 2
    half = length // 2
    lag_rows = 2 * (LAG + 1) * rows
    ahead, back, mean = transform_tables(length)
    operands = (raw, alive, seg_start, norm_half, ahead, back, mean)
    operands = [jnp.asarray(operand) for operand in operands]
    vmem = pl.BlockSpec(memory_space=pltpu.VMEM)
    hbm = pl.BlockSpec(memory_space=pltpu.HBM)
    dma = pltpu.SemaphoreType.DMA
    corr = pl.pallas_call(
        fused_kernel,
        out_shape=pltpu.VMEM((2 * LAG + 1, rows, width * chans), jnp.bfloat16),
        in_specs=[hbm] * 7,
        out_specs=vmem,
        scratch_shapes=[
            pltpu.SMEM((rows,), jnp.int32),
            pltpu.SMEM((segs,), jnp.int32),
            pltpu.SMEM((rows,), jnp.int32),
            dma((3,)),
            dma(()),
            pltpu.VMEM((2, 2, half, half), jnp.bfloat16),
            pltpu.VMEM((2, 2, half, half), jnp.bfloat16),
            pltpu.VMEM((half, half), jnp.bfloat16),
            dma((3,)),
            pltpu.VMEM((groups, 2 * rows, span), jnp.float32),
            pltpu.VMEM((2, 2 * rows, 128), jnp.float32),
            pltpu.VMEM((blocks, 2 * rows, length), jnp.bfloat16),
            pltpu.VMEM((blocks, 2 * rows, length), jnp.bfloat16),
            pltpu.VMEM((2, lag_rows, length), jnp.bfloat16),
            pltpu.VMEM((lag_rows, width * chans), jnp.float32),
            dma((groups - 1,)),
            dma((groups,)),
            dma(()),
            dma(()),
            dma((depth + 1, 3)),
            dma((blocks,)),
            dma((blocks,)),
            dma((blocks,)),
        ],
        compiler_params=pltpu.CompilerParams(
            collective_id=0, has_side_effects=True, vmem_limit_bytes=48 * 1024 * 1024
        ),
        cost_estimate=pl.CostEstimate(
            flops=4 * lag_rows * length * width * chans,
            bytes_accessed=6 * 1024 * 1024,
            transcendentals=0,
        ),
    )(*[pltpu.with_memory_space_constraint(operand, pltpu.HBM) for operand in operands])
    return jnp.transpose(corr, (1, 0, 2))


def on_device(raw, alive, seg_start, norm_half):
    segs, width, span = raw.shape
    shape = (lax.axis_size("chan"), lax.axis_size("tm"), segs, alive.shape[0], span)
    if shape == (8, 4, 2, 8, 256):
        return fused_plan(raw, alive, seg_start, norm_half)
    return gathered_plan(raw, alive, seg_start, norm_half)


def solution(mesh):
    return jax.shard_map(
        on_device,
        mesh=mesh,
        in_specs=(P(None, "chan", "tm"), P(("chan", "tm")), P(), P(("chan", "tm"))),
        out_specs=P(("chan", "tm"), None, None),
        check_vma=False,
    )
```

```python
import math

import jax
import jax.numpy as jnp
import ml_dtypes
import numpy as np
from jax import lax
from jax.experimental import pallas as pl
from jax.experimental.pallas import tpu as pltpu
from jax.sharding import PartitionSpec as P

LAG = 64


widest = 64
smooth_half = 32
tiny = 1e-05
radix = 128


def window_mean(signal, half_width):
    length = signal.shape[2]
    half = half_width[None, :, None]
    width = 2 * half + 1
    power = jnp.pad(jnp.abs(signal), ((0, 0), (0, 0), (widest, widest)))

    def ahead(value, by):
        return jnp.pad(value[:, :, by:], ((0, 0), (0, 0), (0, by)))

    total = jnp.zeros_like(power)
    span = 1
    while span <= 2 * widest + 1:
        total = jnp.where((width & span) != 0, power + ahead(total, span), total)
        power = power + ahead(power, span)
        span *= 2
    rest = widest - half
    span = 1
    while span <= widest:
        total = jnp.where((rest & span) != 0, ahead(total, span), total)
        span *= 2
    return total[:, :, :length] / width.astype(jnp.float32)


def phase_table(row_total, col_total, modulus):
    product = (
        jnp.arange(row_total, dtype=jnp.int32)[:, None]
        * jnp.arange(col_total, dtype=jnp.int32)[None, :]
        % modulus
    )
    angle = product.astype(jnp.float32) * (2.0 * math.pi / modulus)
    return (jnp.cos(angle), jnp.sin(angle))


def forward_transform(signal, cos_q, sin_q, cos_p, sin_p, cos_t, sin_t):
    length = signal.shape[1]
    inner = length // radix
    highest = lax.Precision.HIGHEST
    grid = signal.reshape(-1, inner, radix)
    first_re = jnp.einsum("rqp,qk->rkp", grid, cos_q, precision=highest)
    first_im = -jnp.einsum("rqp,qk->rkp", grid, sin_q, precision=highest)
    turned_re = first_re * cos_t + first_im * sin_t
    turned_im = first_im * cos_t - first_re * sin_t
    out_re = jnp.einsum("rkp,pj->rjk", turned_re, cos_p, precision=highest) + jnp.einsum(
        "rkp,pj->rjk", turned_im, sin_p, precision=highest
    )
    out_im = jnp.einsum("rkp,pj->rjk", turned_im, cos_p, precision=highest) - jnp.einsum(
        "rkp,pj->rjk", turned_re, sin_p, precision=highest
    )
    return (out_re.reshape(-1, length), out_im.reshape(-1, length))


def inverse_real(spec_re, spec_im, cos_q, sin_q, cos_p, sin_p, cos_t, sin_t):
    length = spec_re.shape[1]
    inner = length // radix
    highest = lax.Precision.HIGHEST
    grid_re = spec_re.reshape(-1, radix, inner)
    grid_im = spec_im.reshape(-1, radix, inner)
    first_re = jnp.einsum("rjk,jp->rkp", grid_re, cos_p, precision=highest) - jnp.einsum(
        "rjk,jp->rkp", grid_im, sin_p, precision=highest
    )
    first_im = jnp.einsum("rjk,jp->rkp", grid_im, cos_p, precision=highest) + jnp.einsum(
        "rjk,jp->rkp", grid_re, sin_p, precision=highest
    )
    turned_re = first_re * cos_t - first_im * sin_t
    turned_im = first_im * cos_t + first_re * sin_t
    result = jnp.einsum("rkp,kq->rqp", turned_re, cos_q, precision=highest) - jnp.einsum(
        "rkp,kq->rqp", turned_im, sin_q, precision=highest
    )
    return result.reshape(-1, length)


def whiten(normed):
    segs, rows, length = normed.shape
    inner = length // radix
    cos_q, sin_q = phase_table(inner, inner, inner)
    cos_p, sin_p = phase_table(radix, radix, radix)
    cos_t, sin_t = phase_table(inner, radix, length)
    spec_re, spec_im = forward_transform(
        normed.reshape(-1, length), cos_q, sin_q, cos_p, sin_p, cos_t, sin_t
    )
    magnitude = jnp.sqrt(spec_re * spec_re + spec_im * spec_im)
    circular = jnp.concatenate(
        [magnitude[:, length - smooth_half :], magnitude, magnitude[:, :smooth_half]], axis=1
    )
    running = jnp.cumsum(circular, axis=1)
    running = jnp.concatenate([jnp.zeros((running.shape[0], 1), jnp.float32), running], axis=1)
    span_bins = 2 * smooth_half + 1
    smooth = (running[:, span_bins:] - running[:, :-span_bins]) / span_bins
    bins = jnp.arange(length, dtype=jnp.int32)
    folded = jnp.minimum(bins, length - bins)
    band = ((folded >= length // 250) & (folded <= 2 * length // 5)).astype(jnp.float32)
    gain = band[None, :] / (smooth + tiny)
    traces = inverse_real(spec_re * gain, spec_im * gain, cos_q, sin_q, cos_p, sin_p, cos_t, sin_t)
    return (traces * (1.0 / math.sqrt(length))).reshape(segs, rows, length).astype(jnp.bfloat16)


def normalised(gathered, alive, seg_start, norm_half):
    segs, rows, length = gathered.shape
    gathered = gathered * alive.astype(jnp.float32)[None, :, None]
    pieces = []
    for segment in range(segs):
        padded = jnp.pad(gathered[segment], ((0, 0), (0, length)))
        pieces.append(lax.dynamic_slice_in_dim(padded, seg_start[segment], length, axis=1))
    signal = jnp.stack(pieces, axis=0)
    return signal / (window_mean(signal, norm_half) + tiny)


def gathered_plan(raw, alive, seg_start, norm_half):
    segs = raw.shape[0]
    rows = alive.shape[0]
    lag_count = 2 * LAG + 1
    device = lax.axis_index("chan") * lax.axis_size("tm") + lax.axis_index("tm")
    pieces = lax.all_to_all(raw, "tm", split_axis=1, concat_axis=2, tiled=True)
    white = whiten(normalised(pieces, alive, seg_start, norm_half))
    length = white.shape[2]
    everyone = lax.all_gather(white, ("chan", "tm"), axis=1, tiled=True)
    padded = jnp.pad(white, ((0, 0), (0, 0), (LAG, LAG)))
    toeplitz = jnp.stack(
        [padded[:, :, 2 * LAG - lag : 2 * LAG - lag + length] for lag in range(lag_count)], axis=2
    )
    total = jnp.einsum("silt,sjt->ilj", toeplitz, everyone, preferred_element_type=jnp.float32)
    row_ids = device * rows + jnp.arange(rows, dtype=jnp.int32)
    col_ids = jnp.arange(everyone.shape[1], dtype=jnp.int32)
    keep = row_ids[:, None, None] != col_ids[None, None, :]
    scaled = total * (1.0 / math.sqrt(segs * length))
    return jnp.where(keep, scaled, 0.0).astype(jnp.bfloat16)


MESH = pl.DeviceIdType.MESH


def two_parts(table):
    high = table.astype(ml_dtypes.bfloat16)
    low = (table - high.astype(np.float64)).astype(ml_dtypes.bfloat16)
    return np.stack([high, low])


def transform_tables(length):
    half, quarter = length // 2, length // 4
    moments = np.arange(half)
    low_bin, high_bin = length // 250, 2 * length // 5
    ahead, back = [], []
    for parity in range(2):
        bins = 2 * np.arange(quarter) + parity
        angle = 2.0 * np.pi * ((moments[:, None] * bins[None, :]) % length) / length
        ahead.append(np.concatenate([np.cos(angle), -np.sin(angle)], axis=1))
        back.append(np.concatenate([np.cos(angle), -np.sin(angle)], axis=1).T)
    order = np.concatenate([np.arange(0, half, 2), np.arange(1, half, 2)])
    place = np.empty(half, np.int64)
    place[order] = np.arange(half)
    mean = np.zeros((half, half), np.float32)
    for column, bin_index in enumerate(order):
        if low_bin <= bin_index <= high_bin:
            for offset in range(-smooth_half, smooth_half + 1):
                mean[place[abs(bin_index + offset)], column] += 1.0
    return (
        two_parts(np.stack(ahead)),
        two_parts(np.stack(back)),
        mean.astype(ml_dtypes.bfloat16),
    )


def three_parts(value):
    high = value.astype(jnp.bfloat16)
    rest = value - high.astype(jnp.float32)
    middle = rest.astype(jnp.bfloat16)
    low = (rest - middle.astype(jnp.float32)).astype(jnp.bfloat16)
    return jnp.concatenate([high, middle, low], axis=0)


def split_dot(parts, table):
    rows = parts.shape[0] // 3
    result = jnp.dot(parts, table, preferred_element_type=jnp.float32)
    return result[2 * rows :] + result[rows : 2 * rows] + result[:rows]


def table_dot(value, high, low):
    parts = three_parts(value)
    return split_dot(parts, low) + split_dot(parts, high)


def turned(value, by):
    length = value.shape[1]
    return pltpu.roll(value, by % length, 1)


def window_sum(first, count, limit, way):
    power = first
    total = jnp.where((count & 1) != 0, power, 0.0)
    bit = 1
    while 2 * bit <= limit:
        power = power + turned(power, way * bit)
        bit *= 2
        total = jnp.where((count & bit) != 0, power + turned(total, way * bit), total)
    return total


def normed_rows(records, start, alive, half):
    rows, length = records.shape
    signal = records * jnp.concatenate([alive] * (length // 128), axis=1)
    bit = 1
    while bit <= length // 4:
        digit = (start // bit) % 4
        one, two, three = (turned(signal, -bit * times) for times in (1, 2, 3))
        signal = jnp.where(
            digit == 0, signal, jnp.where(digit == 1, one, jnp.where(digit == 2, two, three))
        )
        bit *= 4
    lane = lax.broadcasted_iota(jnp.int32, (rows, length), 1)
    signal = jnp.where(lane + start < length, signal, 0.0)
    power = jnp.concatenate([jnp.abs(signal), jnp.zeros((rows, 2 * widest), jnp.float32)], axis=1)
    half = jnp.concatenate([half] * (power.shape[1] // 128), axis=1)
    total = window_sum(power, half + 1, widest + 1, -1)
    total = total + window_sum(turned(power, 1), half, widest, 1)
    level = total[:, :length] / (2 * half[:, :length] + 1).astype(jnp.float32)
    return signal / (level + tiny)


def whiten_rows(normed, ahead, back, mean, ready):
    length = normed.shape[1]
    half, quarter = length // 2, length // 4
    left, right = normed[:, :half], normed[:, half:]
    even = table_dot(left + right, ahead[0, 0], ahead[1, 0])
    odd = table_dot(left - right, ahead[0, 1], ahead[1, 1])
    even_power = even * even
    odd_power = odd * odd
    magnitude = jnp.sqrt(
        jnp.concatenate(
            [
                even_power[:, :quarter] + even_power[:, quarter:],
                odd_power[:, :quarter] + odd_power[:, quarter:],
            ],
            axis=1,
        )
    )
    smooth = split_dot(three_parts(magnitude), mean) / (2 * smooth_half + 1)
    place = lax.broadcasted_iota(jnp.int32, smooth.shape, 1)
    bins = jnp.where(place < quarter, 2 * place, 2 * (place - quarter) + 1)
    keep = (bins >= length // 250) & (bins <= 2 * length // 5)
    gain = jnp.where(keep, 1.0 / (smooth + tiny), 0.0)
    even_gain, odd_gain = gain[:, :quarter], gain[:, quarter:]
    even = even * jnp.concatenate([even_gain, even_gain], axis=1)
    odd = odd * jnp.concatenate([odd_gain, odd_gain], axis=1)
    ready()
    even = table_dot(even, back[0, 0], back[1, 0])
    odd = table_dot(odd, back[0, 1], back[1, 1])
    return jnp.concatenate([even + odd, even - odd], axis=1) * (2.0 / math.sqrt(length))


def both_lags(white):
    rows, length = white.shape
    ring = jnp.concatenate([white, jnp.zeros((rows, 2 * LAG), jnp.float32)], axis=1)
    ring = turned(ring, -LAG)
    return jnp.concatenate([ring, turned(ring, 1)], axis=0).astype(jnp.bfloat16)


def fill_lags(both, target, slot, first, last):
    rows = both.shape[0]
    length = target.shape[2]
    for step in range(first, last):
        lagged = turned(both, 2 * step) if step else both
        target[slot, rows * step : rows * (step + 1)] = lagged[:, :length]


def fused_kernel(
    raw, alive_hbm, start_hbm, half_hbm, ahead_hbm, back_hbm, mean_hbm, out,
    alive, seg_start, norm_half, small_sem, own_sem, ahead, back, mean, table_sem, records, params, own, other, lagged, totals,
    raw_send, raw_recv, param_send, param_recv, rail_send, rail_recv, core_send, core_recv,
):
    chan, tm = lax.axis_index("chan"), lax.axis_index("tm")
    depth = lax.axis_size("chan") // 2
    groups = lax.axis_size("tm")
    z, y, x, core = chan // 2, chan % 2, tm // 2, tm % 2
    rows = alive.shape[0]
    pair = 2 * rows
    length = own.shape[2]
    blocks = own.shape[0]

    smalls = [
        pltpu.make_async_copy(source, target, small_sem.at[index])
        for index, (source, target) in enumerate(
            [(alive_hbm, alive), (start_hbm, seg_start), (half_hbm, norm_half)]
        )
    ]
    for load in smalls:
        load.start()
    mine_first = pl.multiple_of(x * pair, pair)
    kept = pltpu.make_async_copy(raw.at[core, pl.ds(mine_first, pair)], records.at[tm], own_sem)
    kept.start()
    loads = [
        pltpu.make_async_copy(source, target, table_sem.at[index])
        for index, (source, target) in enumerate(
            [(ahead_hbm, ahead), (mean_hbm, mean), (back_hbm, back)]
        )
    ]
    for load in loads[:2]:
        load.start()

    near = [z, z + 1 - 2 * (z % 2), z + 2 - 4 * (z // 2), 3 - z]
    others = [(chan, (tm + step) % groups) for step in range(1, groups)]
    along = [(level * 2 + y, tm) for level in near[1:]]
    plane = [
        (y, 1 - x),
        (1 - y, x),
        (1 - y, 1 - x),
    ]
    plane_devices = [(z * 2 + py, px * 2 + core) for py, px in plane]
    barrier = pltpu.get_barrier_semaphore()
    greeted = others + along + plane_devices[1:]
    for device in greeted:
        pl.semaphore_signal(barrier, inc=1, device_id=device, device_id_type=MESH)

    for load in smalls:
        load.wait()
    row_ids = lax.broadcasted_iota(jnp.int32, (rows, 128), 0)
    live = jnp.zeros((rows, 128), jnp.int32)
    half = jnp.zeros((rows, 128), jnp.int32)
    for row in range(rows):
        live = jnp.where(row_ids == row, alive[row], live)
        half = jnp.where(row_ids == row, norm_half[row], half)
    params[core] = jnp.concatenate([live, half], axis=0).astype(jnp.float32)
    pl.semaphore_wait(barrier, len(greeted))

    def remote(source, target, send, receive, device):
        return pltpu.make_async_remote_copy(
            src_ref=source, dst_ref=target, send_sem=send, recv_sem=receive,
            device_id=device, device_id_type=MESH,
        )

    started = []
    for step in range(1, groups):
        peer = (tm + step) % groups
        first = pl.multiple_of((peer // 2) * pair, pair)
        copy = remote(
            raw.at[peer % 2, pl.ds(first, pair)], records.at[tm],
            raw_send.at[step - 1], raw_recv.at[tm], (chan, peer),
        )
        copy.start()
        started.append(copy)
    loads[2].start()
    partner = (chan, x * 2 + 1 - core)
    copy = remote(params.at[core], params.at[core], param_send, param_recv, partner)
    copy.start()
    started.append(copy)
    kept.wait()
    for step in range(1, groups):
        peer = (tm + step) % groups
        remote(
            records.at[peer], records.at[peer], raw_send.at[step - 1], raw_recv.at[peer],
            (chan, peer),
        ).wait_recv()
    remote(
        params.at[1 - core], params.at[1 - core], param_send, param_recv, partner
    ).wait_recv()

    gathered = jnp.concatenate([records[group] for group in range(groups)], axis=1)
    live = jnp.concatenate([params[0, :rows], params[1, :rows]], axis=0)
    half = jnp.concatenate([params[0, rows:], params[1, rows:]], axis=0)
    normed = normed_rows(gathered, seg_start[core], live, half.astype(jnp.int32))
    for load in loads[:2]:
        load.wait()
    white = whiten_rows(normed, ahead, back, mean[...], loads[2].wait).astype(jnp.bfloat16)

    def block_of(bz, by, bx):
        return (bz * 2 + by) * 2 + bx

    def to_core(block):
        copy = remote(
            own.at[block], other.at[block], core_send.at[block], core_recv.at[block], partner
        )
        copy.start()
        started.append(copy)

    def to_side(block, side, semaphore):
        copy = remote(
            own.at[block], own.at[block], semaphore, rail_recv.at[block], plane_devices[side]
        )
        copy.start()
        started.append(copy)

    def to_plane(block, step):
        for side in range(2):
            to_side(block, side, rail_send.at[step, side])

    def arrived(buffer, semaphores, block):
        remote(
            buffer.at[block], buffer.at[block], core_send.at[block], semaphores.at[block], partner
        ).wait_recv()

    mine = block_of(z, y, x)
    own[mine] = white
    for index, device in enumerate(along):
        copy = remote(
            own.at[mine], own.at[mine], rail_send.at[depth, index], rail_recv.at[mine], device
        )
        copy.start()
        started.append(copy)
    to_plane(mine, 0)
    to_core(mine)

    def from_level(step):
        block = block_of(near[step], y, x)
        arrived(own, rail_recv, block)
        to_plane(block, step)
        to_core(block)

    def from_side(step):
        for side in range(2):
            block = block_of(near[step], *plane[side])
            arrived(own, rail_recv, block)
            if step % 2 == side:
                to_side(block, 1 - side, rail_send.at[step, 2])
            to_core(block)

    def own_rows(block):
        wide = block.astype(jnp.float32)
        return both_lags(jnp.where(core == 0, wide[:rows], wide[rows:]))

    both = own_rows(white)
    cuts = [(LAG + 1) * step // (depth - 1) for step in range(depth)]
    for step in range(1, depth):
        fill_lags(both, lagged, 0, cuts[step - 1], cuts[step])
        from_level(step)
    for step in range(2):
        from_side(step)
    arrived(other, core_recv, mine)
    both = own_rows(other[mine])
    fill_lags(both, lagged, 1, 0, LAG // 2)
    for step in range(2, depth):
        from_side(step)
    fill_lags(both, lagged, 1, LAG // 2, LAG + 1)
    for step in range(depth):
        block = block_of(near[step], *plane[2])
        arrived(own, rail_recv, block)
        to_core(block)

    def lag_dot(slot, columns):
        return lax.dot_general(
            lagged[slot],
            columns[...].reshape(blocks * pair, length),
            (((1,), (1,)), ((), ())),
            preferred_element_type=jnp.float32,
        )

    totals[...] = lag_dot(0, own)
    for step in range(depth):
        for py, px in [(y, x)] + plane:
            if step == 0 and px is x and py is y:
                continue
            arrived(other, core_recv, block_of(near[step], py, px))
    lag_count = out.shape[0]
    shape = (rows, blocks * pair)
    ahead_by = lax.broadcasted_iota(jnp.int32, shape, 1) - (chan * groups + tm) * rows
    same = ahead_by == lax.broadcasted_iota(jnp.int32, shape, 0)
    result = (totals[...] + lag_dot(1, other))[: lag_count * rows].reshape(out.shape)
    result = jnp.where(same[None], 0.0, result * (1.0 / math.sqrt(2 * length)))
    out[...] = result.astype(jnp.bfloat16)
    for copy in started:
        copy.wait_send()


def fused_plan(raw, alive, seg_start, norm_half):
    segs, width, span = raw.shape
    groups, chans = lax.axis_size("tm"), lax.axis_size("chan")
    rows = alive.shape[0]
    length = span * groups
    depth = chans // 2
    blocks = chans * 2
    half = length // 2
    lag_rows = 2 * (LAG + 1) * rows
    ahead, back, mean = transform_tables(length)
    operands = (raw, alive, seg_start, norm_half, ahead, back, mean)
    operands = [jnp.asarray(operand) for operand in operands]
    vmem = pl.BlockSpec(memory_space=pltpu.VMEM)
    hbm = pl.BlockSpec(memory_space=pltpu.HBM)
    dma = pltpu.SemaphoreType.DMA
    corr = pl.pallas_call(
        fused_kernel,
        out_shape=pltpu.VMEM((2 * LAG + 1, rows, width * chans), jnp.bfloat16),
        in_specs=[hbm] * 7,
        out_specs=vmem,
        scratch_shapes=[
            pltpu.SMEM((rows,), jnp.int32),
            pltpu.SMEM((segs,), jnp.int32),
            pltpu.SMEM((rows,), jnp.int32),
            dma((3,)),
            dma(()),
            pltpu.VMEM((2, 2, half, half), jnp.bfloat16),
            pltpu.VMEM((2, 2, half, half), jnp.bfloat16),
            pltpu.VMEM((half, half), jnp.bfloat16),
            dma((3,)),
            pltpu.VMEM((groups, 2 * rows, span), jnp.float32),
            pltpu.VMEM((2, 2 * rows, 128), jnp.float32),
            pltpu.VMEM((blocks, 2 * rows, length), jnp.bfloat16),
            pltpu.VMEM((blocks, 2 * rows, length), jnp.bfloat16),
            pltpu.VMEM((2, lag_rows, length), jnp.bfloat16),
            pltpu.VMEM((lag_rows, width * chans), jnp.float32),
            dma((groups - 1,)),
            dma((groups,)),
            dma(()),
            dma(()),
            dma((depth + 1, 3)),
            dma((blocks,)),
            dma((blocks,)),
            dma((blocks,)),
        ],
        compiler_params=pltpu.CompilerParams(
            collective_id=0, has_side_effects=True, vmem_limit_bytes=48 * 1024 * 1024
        ),
        cost_estimate=pl.CostEstimate(
            flops=4 * lag_rows * length * width * chans,
            bytes_accessed=6 * 1024 * 1024,
            transcendentals=0,
        ),
    )(*[pltpu.with_memory_space_constraint(operand, pltpu.HBM) for operand in operands])
    return jnp.transpose(corr, (1, 0, 2))


def on_device(raw, alive, seg_start, norm_half):
    segs, width, span = raw.shape
    shape = (lax.axis_size("chan"), lax.axis_size("tm"), segs, alive.shape[0], span)
    if shape == (8, 4, 2, 8, 256):
        return fused_plan(raw, alive, seg_start, norm_half)
    return gathered_plan(raw, alive, seg_start, norm_half)


def solution(mesh):
    return jax.shard_map(
        on_device,
        mesh=mesh,
        in_specs=(P(None, "chan", "tm"), P(("chan", "tm")), P(), P(("chan", "tm"))),
        out_specs=P(("chan", "tm"), None, None),
        check_vma=False,
    )
```

```python
import math

import jax
import jax.numpy as jnp
import ml_dtypes
import numpy as np
from jax import lax
from jax.experimental import pallas as pl
from jax.experimental.pallas import tpu as pltpu
from jax.sharding import PartitionSpec as P

LAG = 64


widest = 64
smooth_half = 32
tiny = 1e-05
radix = 128


def window_mean(signal, half_width):
    length = signal.shape[2]
    half = half_width[None, :, None]
    width = 2 * half + 1
    power = jnp.pad(jnp.abs(signal), ((0, 0), (0, 0), (widest, widest)))

    def ahead(value, by):
        return jnp.pad(value[:, :, by:], ((0, 0), (0, 0), (0, by)))

    total = jnp.zeros_like(power)
    span = 1
    while span <= 2 * widest + 1:
        total = jnp.where((width & span) != 0, power + ahead(total, span), total)
        power = power + ahead(power, span)
        span *= 2
    rest = widest - half
    span = 1
    while span <= widest:
        total = jnp.where((rest & span) != 0, ahead(total, span), total)
        span *= 2
    return total[:, :, :length] / width.astype(jnp.float32)


def phase_table(row_total, col_total, modulus):
    product = (
        jnp.arange(row_total, dtype=jnp.int32)[:, None]
        * jnp.arange(col_total, dtype=jnp.int32)[None, :]
        % modulus
    )
    angle = product.astype(jnp.float32) * (2.0 * math.pi / modulus)
    return (jnp.cos(angle), jnp.sin(angle))


def forward_transform(signal, cos_q, sin_q, cos_p, sin_p, cos_t, sin_t):
    length = signal.shape[1]
    inner = length // radix
    highest = lax.Precision.HIGHEST
    grid = signal.reshape(-1, inner, radix)
    first_re = jnp.einsum("rqp,qk->rkp", grid, cos_q, precision=highest)
    first_im = -jnp.einsum("rqp,qk->rkp", grid, sin_q, precision=highest)
    turned_re = first_re * cos_t + first_im * sin_t
    turned_im = first_im * cos_t - first_re * sin_t
    out_re = jnp.einsum("rkp,pj->rjk", turned_re, cos_p, precision=highest) + jnp.einsum(
        "rkp,pj->rjk", turned_im, sin_p, precision=highest
    )
    out_im = jnp.einsum("rkp,pj->rjk", turned_im, cos_p, precision=highest) - jnp.einsum(
        "rkp,pj->rjk", turned_re, sin_p, precision=highest
    )
    return (out_re.reshape(-1, length), out_im.reshape(-1, length))


def inverse_real(spec_re, spec_im, cos_q, sin_q, cos_p, sin_p, cos_t, sin_t):
    length = spec_re.shape[1]
    inner = length // radix
    highest = lax.Precision.HIGHEST
    grid_re = spec_re.reshape(-1, radix, inner)
    grid_im = spec_im.reshape(-1, radix, inner)
    first_re = jnp.einsum("rjk,jp->rkp", grid_re, cos_p, precision=highest) - jnp.einsum(
        "rjk,jp->rkp", grid_im, sin_p, precision=highest
    )
    first_im = jnp.einsum("rjk,jp->rkp", grid_im, cos_p, precision=highest) + jnp.einsum(
        "rjk,jp->rkp", grid_re, sin_p, precision=highest
    )
    turned_re = first_re * cos_t - first_im * sin_t
    turned_im = first_im * cos_t + first_re * sin_t
    result = jnp.einsum("rkp,kq->rqp", turned_re, cos_q, precision=highest) - jnp.einsum(
        "rkp,kq->rqp", turned_im, sin_q, precision=highest
    )
    return result.reshape(-1, length)


def whiten(normed):
    segs, rows, length = normed.shape
    inner = length // radix
    cos_q, sin_q = phase_table(inner, inner, inner)
    cos_p, sin_p = phase_table(radix, radix, radix)
    cos_t, sin_t = phase_table(inner, radix, length)
    spec_re, spec_im = forward_transform(
        normed.reshape(-1, length), cos_q, sin_q, cos_p, sin_p, cos_t, sin_t
    )
    magnitude = jnp.sqrt(spec_re * spec_re + spec_im * spec_im)
    circular = jnp.concatenate(
        [magnitude[:, length - smooth_half :], magnitude, magnitude[:, :smooth_half]], axis=1
    )
    running = jnp.cumsum(circular, axis=1)
    running = jnp.concatenate([jnp.zeros((running.shape[0], 1), jnp.float32), running], axis=1)
    span_bins = 2 * smooth_half + 1
    smooth = (running[:, span_bins:] - running[:, :-span_bins]) / span_bins
    bins = jnp.arange(length, dtype=jnp.int32)
    folded = jnp.minimum(bins, length - bins)
    band = ((folded >= length // 250) & (folded <= 2 * length // 5)).astype(jnp.float32)
    gain = band[None, :] / (smooth + tiny)
    traces = inverse_real(spec_re * gain, spec_im * gain, cos_q, sin_q, cos_p, sin_p, cos_t, sin_t)
    return (traces * (1.0 / math.sqrt(length))).reshape(segs, rows, length).astype(jnp.bfloat16)


def normalised(gathered, alive, seg_start, norm_half):
    segs, rows, length = gathered.shape
    gathered = gathered * alive.astype(jnp.float32)[None, :, None]
    pieces = []
    for segment in range(segs):
        padded = jnp.pad(gathered[segment], ((0, 0), (0, length)))
        pieces.append(lax.dynamic_slice_in_dim(padded, seg_start[segment], length, axis=1))
    signal = jnp.stack(pieces, axis=0)
    return signal / (window_mean(signal, norm_half) + tiny)


def gathered_plan(raw, alive, seg_start, norm_half):
    segs = raw.shape[0]
    rows = alive.shape[0]
    lag_count = 2 * LAG + 1
    device = lax.axis_index("chan") * lax.axis_size("tm") + lax.axis_index("tm")
    pieces = lax.all_to_all(raw, "tm", split_axis=1, concat_axis=2, tiled=True)
    white = whiten(normalised(pieces, alive, seg_start, norm_half))
    length = white.shape[2]
    everyone = lax.all_gather(white, ("chan", "tm"), axis=1, tiled=True)
    padded = jnp.pad(white, ((0, 0), (0, 0), (LAG, LAG)))
    toeplitz = jnp.stack(
        [padded[:, :, 2 * LAG - lag : 2 * LAG - lag + length] for lag in range(lag_count)], axis=2
    )
    total = jnp.einsum("silt,sjt->ilj", toeplitz, everyone, preferred_element_type=jnp.float32)
    row_ids = device * rows + jnp.arange(rows, dtype=jnp.int32)
    col_ids = jnp.arange(everyone.shape[1], dtype=jnp.int32)
    keep = row_ids[:, None, None] != col_ids[None, None, :]
    scaled = total * (1.0 / math.sqrt(segs * length))
    return jnp.where(keep, scaled, 0.0).astype(jnp.bfloat16)


MESH = pl.DeviceIdType.MESH


def two_parts(table):
    high = table.astype(ml_dtypes.bfloat16)
    low = (table - high.astype(np.float64)).astype(ml_dtypes.bfloat16)
    return np.stack([high, low])


def transform_tables(length):
    half, quarter = length // 2, length // 4
    moments = np.arange(half)
    low_bin, high_bin = length // 250, 2 * length // 5
    ahead, back = [], []
    for parity in range(2):
        bins = 2 * np.arange(quarter) + parity
        angle = 2.0 * np.pi * ((moments[:, None] * bins[None, :]) % length) / length
        ahead.append(np.concatenate([np.cos(angle), -np.sin(angle)], axis=1))
        back.append(np.concatenate([np.cos(angle), -np.sin(angle)], axis=1).T)
    order = np.concatenate([np.arange(0, half, 2), np.arange(1, half, 2)])
    place = np.empty(half, np.int64)
    place[order] = np.arange(half)
    mean = np.zeros((half, half), np.float32)
    for column, bin_index in enumerate(order):
        if low_bin <= bin_index <= high_bin:
            for offset in range(-smooth_half, smooth_half + 1):
                mean[place[abs(bin_index + offset)], column] += 1.0
    return (
        two_parts(np.stack(ahead)),
        two_parts(np.stack(back)),
        mean.astype(ml_dtypes.bfloat16),
    )


def three_parts(value):
    high = value.astype(jnp.bfloat16)
    rest = value - high.astype(jnp.float32)
    middle = rest.astype(jnp.bfloat16)
    low = (rest - middle.astype(jnp.float32)).astype(jnp.bfloat16)
    return jnp.concatenate([high, middle, low], axis=0)


def split_dot(parts, table):
    rows = parts.shape[0] // 3
    result = jnp.dot(parts, table, preferred_element_type=jnp.float32)
    return result[2 * rows :] + result[rows : 2 * rows] + result[:rows]


def table_dot(value, high, low):
    parts = three_parts(value)
    return split_dot(parts, low) + split_dot(parts, high)


def turned(value, by):
    length = value.shape[1]
    return pltpu.roll(value, by % length, 1)


def window_sum(first, count, limit, way):
    power = first
    total = jnp.where((count & 1) != 0, power, 0.0)
    bit = 1
    while 2 * bit <= limit:
        power = power + turned(power, way * bit)
        bit *= 2
        total = jnp.where((count & bit) != 0, power + turned(total, way * bit), total)
    return total


def normed_rows(records, start, alive, half):
    rows, length = records.shape
    signal = records * jnp.concatenate([alive] * (length // 128), axis=1)
    bit = 1
    while bit <= length // 4:
        digit = (start // bit) % 4
        one, two, three = (turned(signal, -bit * times) for times in (1, 2, 3))
        signal = jnp.where(
            digit == 0, signal, jnp.where(digit == 1, one, jnp.where(digit == 2, two, three))
        )
        bit *= 4
    lane = lax.broadcasted_iota(jnp.int32, (rows, length), 1)
    signal = jnp.where(lane + start < length, signal, 0.0)
    power = jnp.concatenate([jnp.abs(signal), jnp.zeros((rows, 2 * widest), jnp.float32)], axis=1)
    half = jnp.concatenate([half] * (power.shape[1] // 128), axis=1)
    total = window_sum(power, half + 1, widest + 1, -1)
    total = total + window_sum(turned(power, 1), half, widest, 1)
    level = total[:, :length] / (2 * half[:, :length] + 1).astype(jnp.float32)
    return signal / (level + tiny)


def whiten_rows(normed, ahead, back, mean, ready):
    length = normed.shape[1]
    half, quarter = length // 2, length // 4
    left, right = normed[:, :half], normed[:, half:]
    even = table_dot(left + right, ahead[0, 0], ahead[1, 0])
    odd = table_dot(left - right, ahead[0, 1], ahead[1, 1])
    even_power = even * even
    odd_power = odd * odd
    magnitude = jnp.sqrt(
        jnp.concatenate(
            [
                even_power[:, :quarter] + even_power[:, quarter:],
                odd_power[:, :quarter] + odd_power[:, quarter:],
            ],
            axis=1,
        )
    )
    smooth = split_dot(three_parts(magnitude), mean) / (2 * smooth_half + 1)
    place = lax.broadcasted_iota(jnp.int32, smooth.shape, 1)
    bins = jnp.where(place < quarter, 2 * place, 2 * (place - quarter) + 1)
    keep = (bins >= length // 250) & (bins <= 2 * length // 5)
    gain = jnp.where(keep, 1.0 / (smooth + tiny), 0.0)
    even_gain, odd_gain = gain[:, :quarter], gain[:, quarter:]
    even = even * jnp.concatenate([even_gain, even_gain], axis=1)
    odd = odd * jnp.concatenate([odd_gain, odd_gain], axis=1)
    ready()
    even = table_dot(even, back[0, 0], back[1, 0])
    odd = table_dot(odd, back[0, 1], back[1, 1])
    return jnp.concatenate([even + odd, even - odd], axis=1) * (2.0 / math.sqrt(length))


def both_lags(white):
    rows, length = white.shape
    ring = jnp.concatenate([white, jnp.zeros((rows, 2 * LAG), jnp.float32)], axis=1)
    ring = turned(ring, -LAG)
    return jnp.concatenate([ring, turned(ring, 1)], axis=0).astype(jnp.bfloat16)


def fill_lags(both, target, slot, first, last):
    rows = both.shape[0]
    length = target.shape[2]
    for step in range(first, last):
        lagged = turned(both, 2 * step) if step else both
        target[slot, rows * step : rows * (step + 1)] = lagged[:, :length]


def fused_kernel(
    raw, alive_hbm, start_hbm, half_hbm, ahead_hbm, back_hbm, mean_hbm, out,
    alive, seg_start, norm_half, small_sem, own_sem, ahead, back, mean, table_sem, records, params, own, other, lagged, totals,
    raw_send, raw_recv, param_send, param_recv, rail_send, rail_recv, core_send, core_recv,
):
    chan, tm = lax.axis_index("chan"), lax.axis_index("tm")
    depth = lax.axis_size("chan") // 2
    groups = lax.axis_size("tm")
    z, y, x, core = chan // 2, chan % 2, tm // 2, tm % 2
    rows = alive.shape[0]
    pair = 2 * rows
    length = own.shape[2]
    blocks = own.shape[0]

    smalls = [
        pltpu.make_async_copy(source, target, small_sem.at[index])
        for index, (source, target) in enumerate(
            [(alive_hbm, alive), (start_hbm, seg_start), (half_hbm, norm_half)]
        )
    ]
    for load in smalls:
        load.start()
    mine_first = pl.multiple_of(x * pair, pair)
    kept = pltpu.make_async_copy(raw.at[core, pl.ds(mine_first, pair)], records.at[tm], own_sem)
    kept.start()
    loads = [
        pltpu.make_async_copy(source, target, table_sem.at[index])
        for index, (source, target) in enumerate(
            [(ahead_hbm, ahead), (mean_hbm, mean), (back_hbm, back)]
        )
    ]
    for load in loads[:2]:
        load.start()

    near = [z, z + 1 - 2 * (z % 2), z + 2 - 4 * (z // 2), 3 - z]
    others = [(chan, (tm + step) % groups) for step in range(1, groups)]
    along = [(level * 2 + y, tm) for level in near[1:]]
    plane = [
        (y, 1 - x),
        (1 - y, x),
        (1 - y, 1 - x),
    ]
    plane_devices = [(z * 2 + py, px * 2 + core) for py, px in plane]
    barrier = pltpu.get_barrier_semaphore()
    greeted = others + along + plane_devices[1:]
    for device in greeted:
        pl.semaphore_signal(barrier, inc=1, device_id=device, device_id_type=MESH)

    for load in smalls:
        load.wait()
    row_ids = lax.broadcasted_iota(jnp.int32, (rows, 128), 0)
    live = jnp.zeros((rows, 128), jnp.int32)
    half = jnp.zeros((rows, 128), jnp.int32)
    for row in range(rows):
        live = jnp.where(row_ids == row, alive[row], live)
        half = jnp.where(row_ids == row, norm_half[row], half)
    params[core] = jnp.concatenate([live, half], axis=0).astype(jnp.float32)
    pl.semaphore_wait(barrier, len(greeted))

    def remote(source, target, send, receive, device):
        return pltpu.make_async_remote_copy(
            src_ref=source, dst_ref=target, send_sem=send, recv_sem=receive,
            device_id=device, device_id_type=MESH,
        )

    started = []
    for step in range(1, groups):
        peer = (tm + step) % groups
        first = pl.multiple_of((peer // 2) * pair, pair)
        copy = remote(
            raw.at[peer % 2, pl.ds(first, pair)], records.at[tm],
            raw_send.at[step - 1], raw_recv.at[tm], (chan, peer),
        )
        copy.start()
        started.append(copy)
    loads[2].start()
    partner = (chan, x * 2 + 1 - core)
    copy = remote(params.at[core], params.at[core], param_send, param_recv, partner)
    copy.start()
    started.append(copy)
    kept.wait()
    for step in range(1, groups):
        peer = (tm + step) % groups
        remote(
            records.at[peer], records.at[peer], raw_send.at[step - 1], raw_recv.at[peer],
            (chan, peer),
        ).wait_recv()
    remote(
        params.at[1 - core], params.at[1 - core], param_send, param_recv, partner
    ).wait_recv()

    gathered = jnp.concatenate([records[group] for group in range(groups)], axis=1)
    live = jnp.concatenate([params[0, :rows], params[1, :rows]], axis=0)
    half = jnp.concatenate([params[0, rows:], params[1, rows:]], axis=0)
    normed = normed_rows(gathered, seg_start[core], live, half.astype(jnp.int32))
    for load in loads[:2]:
        load.wait()
    white = whiten_rows(normed, ahead, back, mean[...], loads[2].wait).astype(jnp.bfloat16)

    def block_of(bz, by, bx):
        return (bz * 2 + by) * 2 + bx

    def to_core(block):
        copy = remote(
            own.at[block], other.at[block], core_send.at[block], core_recv.at[block], partner
        )
        copy.start()
        started.append(copy)

    def to_side(block, side, semaphore):
        copy = remote(
            own.at[block], own.at[block], semaphore, rail_recv.at[block], plane_devices[side]
        )
        copy.start()
        started.append(copy)

    def to_plane(block, step):
        for side in range(2):
            to_side(block, side, rail_send.at[step, side])

    def arrived(buffer, semaphores, block):
        remote(
            buffer.at[block], buffer.at[block], core_send.at[block], semaphores.at[block], partner
        ).wait_recv()

    mine = block_of(z, y, x)
    own[mine] = white
    for index, device in enumerate(along):
        copy = remote(
            own.at[mine], own.at[mine], rail_send.at[depth, index], rail_recv.at[mine], device
        )
        copy.start()
        started.append(copy)
    to_plane(mine, 0)
    to_core(mine)

    def from_level(step):
        block = block_of(near[step], y, x)
        arrived(own, rail_recv, block)
        to_plane(block, step)
        to_core(block)

    def from_side(step):
        for side in range(2):
            block = block_of(near[step], *plane[side])
            arrived(own, rail_recv, block)
            if step % 2 == side:
                to_side(block, 1 - side, rail_send.at[step, 2])
            to_core(block)

    def own_rows(block):
        wide = block.astype(jnp.float32)
        return both_lags(jnp.where(core == 0, wide[:rows], wide[rows:]))

    both = own_rows(white)
    fill_lags(both, lagged, 0, 0, LAG // 2)
    from_level(1)
    fill_lags(both, lagged, 0, LAG // 2, LAG + 1)
    for step in range(2, depth):
        from_level(step)
    for step in range(3):
        from_side(step)
    arrived(other, core_recv, mine)
    fill_lags(own_rows(other[mine]), lagged, 1, 0, LAG + 1)
    for step in range(3, depth):
        from_side(step)
    for step in range(depth):
        block = block_of(near[step], *plane[2])
        arrived(own, rail_recv, block)
        to_core(block)

    def lag_dot(slot, columns):
        return lax.dot_general(
            lagged[slot],
            columns[...].reshape(blocks * pair, length),
            (((1,), (1,)), ((), ())),
            preferred_element_type=jnp.float32,
        )

    totals[...] = lag_dot(0, own)
    for step in range(depth):
        for py, px in [(y, x)] + plane:
            if step == 0 and px is x and py is y:
                continue
            arrived(other, core_recv, block_of(near[step], py, px))
    lag_count = out.shape[0]
    shape = (rows, blocks * pair)
    ahead_by = lax.broadcasted_iota(jnp.int32, shape, 1) - (chan * groups + tm) * rows
    same = ahead_by == lax.broadcasted_iota(jnp.int32, shape, 0)
    result = (totals[...] + lag_dot(1, other))[: lag_count * rows].reshape(out.shape)
    result = jnp.where(same[None], 0.0, result * (1.0 / math.sqrt(2 * length)))
    out[...] = result.astype(jnp.bfloat16)
    for copy in started:
        copy.wait_send()


def fused_plan(raw, alive, seg_start, norm_half):
    segs, width, span = raw.shape
    groups, chans = lax.axis_size("tm"), lax.axis_size("chan")
    rows = alive.shape[0]
    length = span * groups
    depth = chans // 2
    blocks = chans * 2
    half = length // 2
    lag_rows = 2 * (LAG + 1) * rows
    ahead, back, mean = transform_tables(length)
    operands = (raw, alive, seg_start, norm_half, ahead, back, mean)
    operands = [jnp.asarray(operand) for operand in operands]
    vmem = pl.BlockSpec(memory_space=pltpu.VMEM)
    hbm = pl.BlockSpec(memory_space=pltpu.HBM)
    dma = pltpu.SemaphoreType.DMA
    corr = pl.pallas_call(
        fused_kernel,
        out_shape=pltpu.VMEM((2 * LAG + 1, rows, width * chans), jnp.bfloat16),
        in_specs=[hbm] * 7,
        out_specs=vmem,
        scratch_shapes=[
            pltpu.SMEM((rows,), jnp.int32),
            pltpu.SMEM((segs,), jnp.int32),
            pltpu.SMEM((rows,), jnp.int32),
            dma((3,)),
            dma(()),
            pltpu.VMEM((2, 2, half, half), jnp.bfloat16),
            pltpu.VMEM((2, 2, half, half), jnp.bfloat16),
            pltpu.VMEM((half, half), jnp.bfloat16),
            dma((3,)),
            pltpu.VMEM((groups, 2 * rows, span), jnp.float32),
            pltpu.VMEM((2, 2 * rows, 128), jnp.float32),
            pltpu.VMEM((blocks, 2 * rows, length), jnp.bfloat16),
            pltpu.VMEM((blocks, 2 * rows, length), jnp.bfloat16),
            pltpu.VMEM((2, lag_rows, length), jnp.bfloat16),
            pltpu.VMEM((lag_rows, width * chans), jnp.float32),
            dma((groups - 1,)),
            dma((groups,)),
            dma(()),
            dma(()),
            dma((depth + 1, 3)),
            dma((blocks,)),
            dma((blocks,)),
            dma((blocks,)),
        ],
        compiler_params=pltpu.CompilerParams(
            collective_id=0, has_side_effects=True, vmem_limit_bytes=48 * 1024 * 1024
        ),
        cost_estimate=pl.CostEstimate(
            flops=4 * lag_rows * length * width * chans,
            bytes_accessed=6 * 1024 * 1024,
            transcendentals=0,
        ),
    )(*[pltpu.with_memory_space_constraint(operand, pltpu.HBM) for operand in operands])
    return jnp.transpose(corr, (1, 0, 2))


def on_device(raw, alive, seg_start, norm_half):
    segs, width, span = raw.shape
    shape = (lax.axis_size("chan"), lax.axis_size("tm"), segs, alive.shape[0], span)
    if shape == (8, 4, 2, 8, 256):
        return fused_plan(raw, alive, seg_start, norm_half)
    return gathered_plan(raw, alive, seg_start, norm_half)


def solution(mesh):
    return jax.shard_map(
        on_device,
        mesh=mesh,
        in_specs=(P(None, "chan", "tm"), P(("chan", "tm")), P(), P(("chan", "tm"))),
        out_specs=P(("chan", "tm"), None, None),
        check_vma=False,
    )
```
